32 devices in a mesh: seq: 4 (over z), win: 4 (over y, x), wout: 2 (over core).
Axes of the slice: x: 2, y: 2, z: 4, core: 2. Of those that a mesh axis runs over, the one named last changes fastest.
Arguments:
- qkv_in: bfloat16 [1024, 3, 2048], P('seq', None, ('win', 'wout')), may hold values from -6 to 6
- conv_w: float32 [3, 4, 2048], P(None, None, ('win', 'wout')), may hold values from -3 to 3
- beta_logits: float32 [16, 1024], P(('win', 'wout'), 'seq'), may hold values from -10 to 3
- lengths: int32 [4], replicated, may hold values from 1 to 384, as said below
- out_gain: float32 [128], replicated, may hold values from 0.1 to 1.9
- w_out: bfloat16 [2048, 2048], P(('win', 'wout')), may hold values from -0.125 to 0.125
- hidden_in: bfloat16 [1024, 2048], P(('seq', 'win', 'wout')), may hold values from -6 to 6
- norm_gain: float32 [2048], replicated, may hold values from 0.1 to 1.9
- w_qkv: bfloat16 [2048, 6144], P('win', 'wout'), may hold values from -0.125 to 0.125
Outputs:
- qkv_next: bfloat16 [1024, 6144], P(('seq', 'win'), 'wout')
- stream_out: bfloat16 [1024, 2048], P(('seq', 'win', 'wout'))
- final_states: float32 [4, 16, 128, 128], P(None, ('win', 'wout'))
- conv_edges: bfloat16 [4, 3, 3, 2048], P(None, None, None, ('win', 'wout'))
The draws below stay inside these ranges and needn't reach their ends.
Inputs may be any that keep to these rules, and one draw needn't show every extreme that they name: The lengths sum to 1024; the largest is exactly 384.
All inputs are finite; a program needn't handle non-finite values.
Results may differ from the reference program's by a relative error of at most 0.022.
Values may be sent and summed in bfloat16 or wider, within the bound.
A program may use at most 64 MiB of HBM per device.

```python
import jax
import jax.numpy as jnp
from jax import lax

D = 2048
H = 16
DK = 128
CONV = 4
TOK_DEV = 256
REQS = 4
HD = 2048
PROMPT_LENGTH_SUM = 1024
MOST = 384
N_SEQ = 4


def draw_lengths(key, part):
    first_key = jax.random.fold_in(key, 11)
    second_key = jax.random.fold_in(key, 23)
    first = jax.random.randint(first_key, (), TOK_DEV + 1, min(2 * TOK_DEV, MOST) + 1)
    end_second = jax.random.randint(second_key, (), PROMPT_LENGTH_SUM // 2 + 1, PROMPT_LENGTH_SUM // 2 + TOK_DEV // 2)
    third = PROMPT_LENGTH_SUM - MOST - end_second
    last = jnp.int32(MOST)
    return jnp.stack([first, end_second - first, third, last]).astype(jnp.int32)


def draw_beta_logits(key, part):
    lookup_vectors = jax.random.split(key, 6)
    slow = jax.random.randint(lookup_vectors[0], (H,), 0, 2) > 0
    slow_rate = jax.random.uniform(lookup_vectors[1], (H,), minval=0.1, maxval=0.6) * (DK / MOST)
    fast_rate = jax.random.uniform(lookup_vectors[2], (H,), minval=0.2, maxval=0.8)
    rate = jnp.where(slow, slow_rate, fast_rate)
    block_count = PROMPT_LENGTH_SUM // TOK_DEV
    block_factor = jnp.exp(jax.random.uniform(lookup_vectors[3], (H, block_count), minval=-0.7, maxval=0.7))
    block_factor = jnp.repeat(block_factor, TOK_DEV, axis=1)
    token_factor = jnp.exp(jax.random.uniform(lookup_vectors[4], (H, PROMPT_LENGTH_SUM), minval=-0.7, maxval=0.7))
    beta_coefficient = jnp.clip(rate[:, None] * block_factor * token_factor, 5e-05, 0.95)
    position_group = jax.random.uniform(lookup_vectors[5], (PROMPT_LENGTH_SUM,)) < 8.0 / PROMPT_LENGTH_SUM
    beta_coefficient = jnp.where(position_group[None, :], 0.6, beta_coefficient)
    return (jnp.log(beta_coefficient) - jnp.log1p(-beta_coefficient)).astype(jnp.float32)


def shard_levels(stream_key, extent, cuts, smallest, largest):
    level = 1.0
    for position, shards_of in cuts:
        steps = jax.random.uniform(jax.random.fold_in(jax.random.fold_in(stream_key, 6), position), (shards_of,), jnp.float32, smallest / len(cuts), largest / len(cuts))
        level = level * jnp.repeat(jnp.exp(steps), extent[position] // shards_of).reshape((-1,) + (1,) * (len(extent) - 1 - position))
    return level


def noise(stream_key, shape, spread, reach, pieces=(), kind=jnp.bfloat16):
    level = shard_levels(stream_key, shape, pieces, -0.22, 0.18) if pieces else 1.0
    entries = jax.random.normal(stream_key, shape, jnp.float32) * spread * level
    return jnp.minimum(jnp.maximum(entries, -reach), reach).astype(kind)


def setup_inputs(seed: int = 0) -> dict:
    keys = jax.random.split(jax.random.key(seed), 10)
    qkv_in = noise(keys[0], (PROMPT_LENGTH_SUM, 3, HD), 1.0, 6.0, ((0, 4), (2, 8)))
    conv_w = noise(keys[1], (3, CONV, HD), CONV ** -0.5, 3.0, ((2, 8),), jnp.float32)
    beta_logits = draw_beta_logits(jax.random.fold_in(keys[9], 71), 0)
    lengths = draw_lengths(jax.random.fold_in(keys[9], 71), 0)
    out_gain = jnp.clip(1.0 + 0.18 * jax.random.normal(keys[4], (DK,), jnp.float32), 0.1, 1.9)
    w_out = noise(keys[5], (HD, D), HD ** -0.5, 0.125, ((0, 8),))
    hidden_in = noise(keys[6], (PROMPT_LENGTH_SUM, D), 1.0, 6.0, ((0, 32),))
    norm_gain = jnp.clip(1.0 + 0.18 * jax.random.normal(keys[7], (D,), jnp.float32), 0.1, 1.9)
    w_qkv = noise(keys[8], (D, 3 * D), D ** -0.5, 0.125, ((0, 4), (1, 2)))
    return dict(qkv_in=qkv_in, conv_w=conv_w, beta_logits=beta_logits, lengths=lengths, out_gain=out_gain, w_out=w_out, hidden_in=hidden_in, norm_gain=norm_gain, w_qkv=w_qkv)


def segment_ids(positions, seg_ends):
    counts = lax.optimization_barrier(jnp.sum((positions[:, None] >= seg_ends[None, :]).astype(jnp.int32), axis=1))
    return jnp.where(positions < 0, -1, counts).astype(jnp.int32)

def unit_rows(values):
    return values / jnp.sqrt(lax.optimization_barrier(jnp.sum(values * values, axis=-1, keepdims=True)) + 1e-06)

def reference(qkv_in, conv_w, beta_logits, lengths, out_gain, w_out, hidden_in, norm_gain, w_qkv):
    seg_ends = jnp.cumsum(lengths).astype(jnp.int32)
    positions = jnp.arange(PROMPT_LENGTH_SUM, dtype=jnp.int32)
    segment = segment_ids(positions, seg_ends)
    inputs_wide = qkv_in.astype(jnp.float32)
    pre = jnp.zeros((PROMPT_LENGTH_SUM, 3, HD), jnp.float32)
    for offset in range(CONV):
        shift_by = CONV - 1 - offset
        moved = jnp.concatenate([jnp.zeros((shift_by, 3, HD), jnp.float32), inputs_wide[:PROMPT_LENGTH_SUM - shift_by]], axis=0)
        moved_seg = jnp.concatenate([jnp.full((shift_by,), -1, jnp.int32), segment[:PROMPT_LENGTH_SUM - shift_by]], axis=0)
        same_request = (moved_seg == segment).astype(jnp.float32)
        pre = pre + conv_w[:, offset, :][None] * moved * same_request[:, None, None]
    activated = jax.nn.silu(pre).astype(jnp.bfloat16)
    query = unit_rows(activated[:, 0].astype(jnp.float32).reshape(PROMPT_LENGTH_SUM, H, DK))
    keys_all = unit_rows(activated[:, 1].astype(jnp.float32).reshape(PROMPT_LENGTH_SUM, H, DK))
    values_all = activated[:, 2].astype(jnp.float32).reshape(PROMPT_LENGTH_SUM, H, DK)
    beta_coefficient = jax.nn.sigmoid(beta_logits).T

    def token_step(carried_state, inputs):
        memory_state, previous, finished = carried_state
        query_t, key_t, value_t, strength_t, segment_t = inputs
        boundary = (segment_t != previous) & (previous >= 0)
        slot = jnp.maximum(previous, 0)
        finished = finished.at[slot].set(jnp.where(boundary, memory_state, finished[slot]))
        prior = jnp.where(segment_t == previous, memory_state, jnp.zeros_like(memory_state))
        predicted = lax.optimization_barrier(jnp.sum(prior * key_t[:, :, None], axis=1))
        memory_state = prior + strength_t[:, None, None] * key_t[:, :, None] * (value_t - predicted)[:, None, :]
        attended_t = lax.optimization_barrier(jnp.sum(memory_state * query_t[:, :, None], axis=1))
        return ((memory_state, segment_t, finished), attended_t)
    start = (jnp.zeros((H, DK, DK), jnp.float32), jnp.int32(-1), jnp.zeros((REQS, H, DK, DK), jnp.float32))
    (memory_state, previous, finished), attended = lax.scan(token_step, start, (query, keys_all, values_all, beta_coefficient, segment))
    final_states = finished.at[REQS - 1].set(memory_state)
    rim_rows = CONV - 1
    last_tok = seg_ends - 1
    wanted = last_tok[:, None] - rim_rows + 1 + jnp.arange(rim_rows, dtype=jnp.int32)[None, :]
    valid = wanted >= (seg_ends - lengths)[:, None]
    picked = qkv_in[jnp.clip(wanted, 0, PROMPT_LENGTH_SUM - 1)]
    conv_edges = jnp.where(valid[:, :, None, None], picked, jnp.zeros_like(picked))
    scale_heads = jnp.sqrt(lax.optimization_barrier(jnp.mean(attended * attended, axis=-1, keepdims=True)) + 1e-05)
    normed_heads = (attended / scale_heads * out_gain).reshape(PROMPT_LENGTH_SUM, HD).astype(jnp.bfloat16)
    mixed = jnp.dot(normed_heads, w_out, preferred_element_type=jnp.float32)
    summed = hidden_in.astype(jnp.float32) + mixed
    stream_out = summed.astype(jnp.bfloat16)
    scale_stream = jnp.sqrt(lax.optimization_barrier(jnp.mean(summed * summed, axis=-1, keepdims=True)) + 1e-05)
    normed_stream = (summed / scale_stream * norm_gain).astype(jnp.bfloat16)

    def project(rows_block):
        return jnp.dot(rows_block, w_qkv, preferred_element_type=jnp.float32).astype(jnp.bfloat16)
    qkv_next = lax.map(project, normed_stream.reshape(N_SEQ, TOK_DEV, D)).reshape(PROMPT_LENGTH_SUM, 3 * D)
    return (qkv_next, stream_out, final_states, conv_edges)
```

```python
import functools

import jax
import jax.numpy as jnp
from jax import lax
from jax.experimental import pallas as pl
from jax.experimental.pallas import tpu as pltpu
from jax.sharding import PartitionSpec as P

MESH = pl.DeviceIdType.MESH
DK = 128
CONV = 4
HALO = 16
F32 = jnp.float32
BF16 = jnp.bfloat16


def dot(a, b):
    return jnp.dot(a, b, preferred_element_type=F32)


def dot_t(a, b):
    return lax.dot_general(a, b, (((1,), (1,)), ((), ())), preferred_element_type=F32)


def split(x):
    high = x.astype(BF16)
    return high, (x - high.astype(F32)).astype(BF16)


def mm3(a, b, product=dot):
    ah, al = split(a)
    bh, bl = split(b)
    return product(ah, bh) + (product(ah, bl) + product(al, bh))


def kernel(
    n, wins, reqs,
    lengths, qkv, conv_w, beta, out_gain, hidden, norm_gain, w_out, w_qkv,
    qkv_next, stream_out, fs_out, edge_out,
    halo, wo_own, wo_sib, wq, state_send, state_recv, nh, nh_send, nh_recv,
    part_keep, part_send, part_recv, ns, gathered, proj_send, proj_recv,
    res, up_send, up_recv, down_send, down_recv,
    local_sem, halo_sem, wo_sem, state_sem, nh_sem, part_send_sem, part_recv_sem,
    ns_send_sem, ns_recv_sem, proj_send_sem, proj_recv_sem, up_sem, down_sem,
):
    rows = qkv.shape[1]
    width = qkv.shape[2]
    heads = width // DK
    half = rows // 2
    group = wins * 2
    blk = hidden.shape[0]
    k_idx = lax.axis_index("seq")
    w = lax.axis_index("win")
    c = lax.axis_index("wout")
    me = w * 2 + c
    sib = {"wout": 1 - c}
    above = {"seq": lax.rem(k_idx + 1, n)}
    below = {"seq": lax.rem(k_idx + n - 1, n)}
    not_first = k_idx > 0
    not_last = k_idx < n - 1

    def remote(src, dst, send_sem, recv_sem, device):
        return pltpu.make_async_remote_copy(
            src_ref=src, dst_ref=dst, send_sem=send_sem, recv_sem=recv_sem,
            device_id=device, device_id_type=MESH,
        )

    def peer(o):
        p = lax.rem(me + o, group)
        return p // 2, lax.rem(p, 2)

    barrier = pltpu.get_barrier_semaphore()
    for o in range(1, group):
        pw, pc = peer(o)
        pl.semaphore_signal(barrier, inc=1, device_id={"win": pw, "wout": pc}, device_id_type=MESH)

    @pl.when(not_first)
    def _():
        pl.semaphore_signal(barrier, inc=1, device_id=below, device_id_type=MESH)

    @pl.when(not_last)
    def _():
        pl.semaphore_signal(barrier, inc=1, device_id=above, device_id_type=MESH)

    copy_wo = pltpu.make_async_copy(w_out, wo_own, local_sem.at[0])
    copy_wq = pltpu.make_async_copy(w_qkv, wq, local_sem.at[1])
    copy_wo.start()
    copy_wq.start()
    pl.semaphore_wait(
        barrier, group - 1 + not_first.astype(jnp.int32) + not_last.astype(jnp.int32)
    )

    halo_copy = remote(
        qkv.at[:, pl.ds(rows - HALO, HALO), :], halo, halo_sem.at[0], halo_sem.at[1], above
    )

    @pl.when(not_last)
    def _():
        halo_copy.start()

    wo_copy = remote(w_out, wo_sib, wo_sem.at[0], wo_sem.at[1], sib)
    wo_copy.start()

    @pl.when(jnp.logical_not(not_first))
    def _():
        halo[...] = jnp.zeros_like(halo)
        state_recv[...] = jnp.zeros_like(state_recv)

    ends = []
    total = jnp.int32(0)
    for r in range(reqs):
        total = total + lengths[r]
        ends.append(total)
    first = k_idx * rows

    def segments(positions):
        seg = jnp.zeros_like(positions)
        for r in range(reqs):
            seg = seg + (positions >= ends[r]).astype(jnp.int32)
        return jnp.where(positions < 0, -1, seg)

    def scalar_segment(position):
        seg = jnp.int32(0)
        for r in range(reqs):
            seg = seg + (position >= ends[r]).astype(jnp.int32)
        return jnp.where(position < 0, -1, seg)

    col_pos = first + lax.broadcasted_iota(jnp.int32, (rows, 1), 0)
    row_pos = first + lax.broadcasted_iota(jnp.int32, (1, rows), 1)
    col_seg = segments(col_pos)
    row_seg = segments(row_pos)
    before_seg = scalar_segment(first - 1)
    last_seg = scalar_segment(first + rows - 1)
    coupled = (col_seg == before_seg).astype(F32)
    in_last = (row_seg == last_seg).astype(F32)
    last_link = (before_seg == last_seg).astype(F32)

    ri = lax.broadcasted_iota(jnp.int32, (rows, rows), 0)
    ci = lax.broadcasted_iota(jnp.int32, (rows, rows), 1)
    same = col_seg == row_seg
    causal = same & (ri >= ci)
    strict = same & (ri > ci)
    diagonal = ri == ci
    hi_ = lax.broadcasted_iota(jnp.int32, (half, half), 0)
    hj_ = lax.broadcasted_iota(jnp.int32, (half, half), 1)
    eye_half = (hi_ == hj_).astype(F32)
    eye_keys = (
        lax.broadcasted_iota(jnp.int32, (DK, DK), 0) == lax.broadcasted_iota(jnp.int32, (DK, DK), 1)
    ).astype(F32)

    @pl.when(not_first)
    def _():
        halo_copy.wait_recv()

    activated = []
    extended = []
    for t in range(3):
        ext = jnp.concatenate([halo[t], qkv[t]], axis=0)
        extended.append(ext)
        wide = ext.astype(F32)
        pre = conv_w[t, CONV - 1 : CONV, :] * wide[HALO:]
        for back in range(1, CONV):
            shifted = pltpu.roll(wide, back, axis=0)[HALO:]
            keep = segments(col_pos - back) == col_seg
            pre = pre + conv_w[t, CONV - 1 - back : CONV - back, :] * jnp.where(keep, shifted, 0.0)
        activated.append((pre / (1.0 + jnp.exp(-pre))).astype(BF16).astype(F32))

    def unit(x):
        return x * lax.rsqrt(jnp.sum(x * x, axis=-1, keepdims=True) + 1e-6)

    q, k, v, kt, a_full, scores, strength = [], [], [], [], [], [], []
    for h in range(heads):
        cols = slice(h * DK, (h + 1) * DK)
        q.append(unit(activated[0][:, cols]))
        k.append(unit(activated[1][:, cols]))
        v.append(activated[2][:, cols])
        b_row = 1.0 / (1.0 + jnp.exp(-beta[h : h + 1, :]))
        b_col = jnp.sum(jnp.where(diagonal, b_row, 0.0), axis=1, keepdims=True)
        strength.append(b_col)
        kt.append(jnp.transpose(k[h]))
        gram = mm3(k[h], k[h], dot_t)
        a_full.append(jnp.where(strict, b_col * gram, 0.0))
        scores.append(jnp.where(causal, mm3(q[h], k[h], dot_t), 0.0))

    diag = []
    for h in range(heads):
        diag.append(a_full[h][:half, :half])
        diag.append(a_full[h][half:, half:])
    level = 0
    inverse = None
    while (1 << level) < half:
        pick = (
            ((hi_ >> (level + 1)) == (hj_ >> (level + 1)))
            & (((hi_ >> level) & 1) == 1)
            & (((hj_ >> level) & 1) == 0)
        )
        lower = [jnp.where(pick, a, 0.0) for a in diag]
        if level == 0:
            inverse = [eye_half - x for x in lower]
        else:
            ys = [mm3(x, z) for x, z in zip(lower, inverse)]
            inverse = [z - mm3(z, y) for z, y in zip(inverse, ys)]
        level += 1

    solved, out_local, q_link, trans, write = [], [], [], [], []
    for h in range(heads):
        rhs = jnp.concatenate([strength[h] * v[h], (strength[h] * coupled) * k[h]], axis=1)
        top = mm3(inverse[2 * h], rhs[:half])
        low = mm3(inverse[2 * h + 1], rhs[half:] - mm3(a_full[h][half:, :half], top))
        solved.append(jnp.concatenate([top, low], axis=0))
    for h in range(heads):
        m = mm3(kt[h] * in_last, solved[h])
        write.append(m[:, :DK])
        trans.append(last_link * (eye_keys - m[:, DK:]))

    state_copy = remote(state_send, state_recv, state_sem.at[0], state_sem.at[1], above)

    @pl.when(not_first)
    def _():
        state_copy.wait_recv()

    state_in = [state_recv[h * DK : (h + 1) * DK, :].astype(F32) for h in range(heads)]
    for h in range(heads):
        state_send[h * DK : (h + 1) * DK, :] = (mm3(trans[h], state_in[h]) + write[h]).astype(BF16)

    @pl.when(not_last)
    def _():
        state_copy.start()

    corrected = []
    for h in range(heads):
        s = mm3(scores[h], solved[h])
        link = jnp.concatenate([coupled * q[h] - s[:, DK:], solved[h][:, DK:]], axis=0)
        applied = mm3(link, state_in[h])
        att = s[:, :DK] + applied[:rows]
        corrected.append(solved[h][:, :DK] - applied[rows:])
        scale = lax.rsqrt(jnp.mean(att * att, axis=-1, keepdims=True) + 1e-5)
        nh[:, h * DK : (h + 1) * DK] = (att * scale * out_gain[...]).astype(BF16)

    for o in range(wins):
        start = pl.multiple_of((2 * o + 1 - c) * blk, blk)
        nh_send[o * blk : (o + 1) * blk, :] = nh[pl.ds(start, blk), :]
    nh_copy = remote(nh_send, nh_recv, nh_sem.at[0], nh_sem.at[1], sib)
    nh_copy.start()
    own_rows = jnp.concatenate(
        [nh[pl.ds(pl.multiple_of((2 * o + c) * blk, blk), blk), :] for o in range(wins)], axis=0
    )
    copy_wo.wait()
    wo_copy.wait_recv()
    part_keep[...] = dot(own_rows, wo_own[...])
    nh_copy.wait_recv()
    part_keep[...] = part_keep[...] + dot(nh_recv[...], wo_sib[...])
    part_copies = []
    for o in range(1, wins):
        pw = lax.rem(w + o, wins)
        part_send[o] = part_keep[pl.ds(pl.multiple_of(pw * blk, blk), blk), :].astype(BF16)
        cp = remote(
            part_send.at[o], part_recv.at[o], part_send_sem.at[o], part_recv_sem.at[o], {"win": pw}
        )
        cp.start()
        part_copies.append(cp)

    for r in range(reqs):
        owned = (ends[r] - 1 >= first) & (ends[r] - 1 < first + rows)
        owned_f = owned.astype(F32)
        member = (row_seg == r).astype(F32) * owned_f
        carry = owned_f * (before_seg == r).astype(F32)
        for h in range(heads):
            base = (r * heads + h) * DK
            res[base : base + DK, :] = (
                mm3(kt[h] * member, corrected[h]) + carry * state_in[h]
            ).astype(BF16)
    edge_base = reqs * heads * DK
    sel_row = lax.broadcasted_iota(jnp.int32, (16, HALO + rows), 0)
    sel_pos = first - HALO + lax.broadcasted_iota(jnp.int32, (16, HALO + rows), 1)
    sel_seg = segments(sel_pos)
    select = jnp.zeros((16, HALO + rows), F32)
    for r in range(reqs):
        owned = (ends[r] - 1 >= first) & (ends[r] - 1 < first + rows)
        for i in range(CONV - 1):
            hit = (
                (sel_row == r * (CONV - 1) + i)
                & (sel_pos == ends[r] - (CONV - 1) + i)
                & (sel_seg == r)
            )
            select = select + jnp.where(hit, 1.0, 0.0) * owned.astype(F32)
    select = select.astype(BF16)
    pieces = width // DK
    for t in range(3):
        edge = dot(select, extended[t])
        for j in range(pieces):
            base = edge_base + (t * pieces + j) * 16
            res[base : base + 16, :] = edge[:, j * DK : (j + 1) * DK].astype(BF16)

    up_copy = remote(up_send, up_recv, up_sem.at[0], up_sem.at[1], above)
    down_copy = remote(down_send, down_recv, down_sem.at[0], down_sem.at[1], below)

    def up_step():
        up_copy.wait_recv()

        @pl.when(not_last)
        def _():
            up_send[...] = up_recv[...] + res[...]
            up_copy.start()

    def down_step():
        down_copy.wait_recv()

        @pl.when(not_first)
        def _():
            down_send[...] = down_recv[...] + res[...]
            down_copy.start()

    @pl.when(k_idx == 0)
    def _():
        up_recv[...] = jnp.zeros_like(up_recv)
        up_send[...] = res[...]
        up_copy.start()

    @pl.when(k_idx == n - 1)
    def _():
        down_recv[...] = jnp.zeros_like(down_recv)
        down_send[...] = res[...]
        down_copy.start()

    summed = hidden[...].astype(F32) + part_keep[pl.ds(pl.multiple_of(w * blk, blk), blk), :]
    for o in range(1, wins):
        part_copies[o - 1].wait_recv()
        summed = summed + part_recv[o].astype(F32)
    stream_out[...] = summed.astype(BF16)
    scale = lax.rsqrt(jnp.mean(summed * summed, axis=-1, keepdims=True) + 1e-5)
    ns[...] = (summed * scale * norm_gain[...]).astype(BF16)
    in_block = wq.shape[0]
    my_rows = pl.ds(pl.multiple_of(me * blk, blk), blk)
    ns_copies = []
    for o in range(1, group):
        pw, pc = peer(o)
        cp = remote(
            ns.at[:, pl.ds(pl.multiple_of(pw * in_block, in_block), in_block)],
            gathered.at[my_rows, :],
            ns_send_sem.at[o], ns_recv_sem.at[o], {"win": pw, "wout": pc},
        )
        cp.start()
        ns_copies.append(cp)
    gathered[my_rows, :] = ns[:, pl.ds(pl.multiple_of(w * in_block, in_block), in_block)]

    pl.when(k_idx == 1)(up_step)
    pl.when(k_idx == n - 2)(down_step)

    copy_wq.wait()
    for cp in ns_copies:
        cp.wait_recv()
    out_rows = blk * 2
    proj_copies = []
    for o in range(1, wins):
        pw = lax.rem(w + o, wins)
        block = gathered[pl.ds(pl.multiple_of(pw * out_rows, out_rows), out_rows), :]
        proj_send[o] = dot(block, wq[...]).astype(BF16)
        cp = remote(
            proj_send.at[o], proj_recv.at[o], proj_send_sem.at[o], proj_recv_sem.at[o], {"win": pw}
        )
        cp.start()
        proj_copies.append(cp)
    own = dot(gathered[pl.ds(pl.multiple_of(w * out_rows, out_rows), out_rows), :], wq[...])

    pl.when((k_idx == 2) & (k_idx > 1))(up_step)
    pl.when((k_idx == n - 3) & (k_idx < n - 2))(down_step)
    pl.when(k_idx > 2)(up_step)
    pl.when(k_idx < n - 3)(down_step)

    total_res = res[...].astype(F32) + up_recv[...].astype(F32) + down_recv[...].astype(F32)
    fs_out[...] = total_res[:edge_base]
    for t in range(3 * pieces):
        base = edge_base + t * 16
        edge_out[:, t * DK : (t + 1) * DK] = total_res[base : base + 16].astype(BF16)

    for cp in proj_copies:
        cp.wait_recv()
    for o in range(1, wins):
        own = own + proj_recv[o].astype(F32)
    qkv_next[...] = own.astype(BF16)

    wo_copy.wait_send()
    nh_copy.wait_send()
    for cp in part_copies + ns_copies + proj_copies:
        cp.wait_send()

    @pl.when(not_last)
    def _():
        halo_copy.wait_send()
        state_copy.wait_send()
        up_copy.wait_send()

    @pl.when(not_first)
    def _():
        down_copy.wait_send()


def solution(mesh):
    n, wins = mesh.shape["seq"], mesh.shape["win"]

    def body(qkv_in, conv_w, beta_logits, lengths, out_gain, w_out, hidden_in, norm_gain, w_qkv):
        rows, _, width = qkv_in.shape
        heads = width // DK
        reqs = lengths.shape[0]
        blk, model = hidden_in.shape
        in_block, out_cols = w_qkv.shape
        group = wins * 2
        res_rows = reqs * heads * DK + 16 * 3 * (width // DK)
        vmem = pl.BlockSpec(memory_space=pltpu.VMEM)
        dma = pltpu.SemaphoreType.DMA
        results = pl.pallas_call(
            functools.partial(kernel, n, wins, reqs),
            out_shape=(
                jax.ShapeDtypeStruct((blk * 2, out_cols), BF16),
                jax.ShapeDtypeStruct((blk, model), BF16),
                jax.ShapeDtypeStruct((reqs * heads * DK, DK), F32),
                jax.ShapeDtypeStruct((16, 3 * width), BF16),
            ),
            in_specs=[pl.BlockSpec(memory_space=pltpu.SMEM)] + [vmem] * 6
            + [pl.BlockSpec(memory_space=pl.ANY)] * 2,
            out_specs=(vmem,) * 4,
            scratch_shapes=[
                pltpu.VMEM((3, HALO, width), BF16),
                pltpu.VMEM((width, model), BF16),
                pltpu.VMEM((width, model), BF16),
                pltpu.VMEM((in_block, out_cols), BF16),
                pltpu.VMEM((heads * DK, DK), BF16),
                pltpu.VMEM((heads * DK, DK), BF16),
                pltpu.VMEM((rows, width), BF16),
                pltpu.VMEM((rows // 2, width), BF16),
                pltpu.VMEM((rows // 2, width), BF16),
                pltpu.VMEM((rows // 2, model), F32),
                pltpu.VMEM((wins, blk, model), BF16),
                pltpu.VMEM((wins, blk, model), BF16),
                pltpu.VMEM((blk, model), BF16),
                pltpu.VMEM((rows, in_block), BF16),
                pltpu.VMEM((wins, blk * 2, out_cols), BF16),
                pltpu.VMEM((wins, blk * 2, out_cols), BF16),
                pltpu.VMEM((res_rows, DK), BF16),
                pltpu.VMEM((res_rows, DK), BF16),
                pltpu.VMEM((res_rows, DK), BF16),
                pltpu.VMEM((res_rows, DK), BF16),
                pltpu.VMEM((res_rows, DK), BF16),
                dma((2,)), dma((2,)), dma((2,)), dma((2,)), dma((2,)),
                dma((wins,)), dma((wins,)), dma((group,)), dma((group,)),
                dma((wins,)), dma((wins,)), dma((2,)), dma((2,)),
            ],
            compiler_params=pltpu.CompilerParams(
                collective_id=0, has_side_effects=True, vmem_limit_bytes=56 * 1024 * 1024
            ),
            cost_estimate=pl.CostEstimate(
                flops=4 * 10**9, bytes_accessed=8 * 10**6, transcendentals=10**6
            ),
            name="delta_sublayer",
        )(
            lengths, jnp.transpose(qkv_in, (1, 0, 2)), conv_w, beta_logits,
            out_gain.reshape(1, DK), hidden_in, norm_gain.reshape(1, model), w_out, w_qkv,
        )
        projected, stream, states, edges = results
        taps = CONV - 1
        return (
            projected,
            stream,
            states.reshape(reqs, heads, DK, DK),
            edges[: reqs * taps].reshape(reqs, taps, 3, width),
        )

    return jax.shard_map(
        body,
        mesh=mesh,
        in_specs=(
            P("seq", None, ("win", "wout")),
            P(None, None, ("win", "wout")),
            P(("win", "wout"), "seq"),
            P(),
            P(),
            P(("win", "wout"), None),
            P(("seq", "win", "wout"), None),
            P(),
            P("win", "wout"),
        ),
        out_specs=(
            P(("seq", "win"), "wout"),
            P(("seq", "win", "wout"), None),
            P(None, ("win", "wout"), None, None),
            P(None, None, None, ("win", "wout")),
        ),
        check_vma=False,
    )
```

```python
import functools

import jax
import jax.numpy as jnp
from jax import lax
from jax.experimental import pallas as pl
from jax.experimental.pallas import tpu as pltpu
from jax.sharding import PartitionSpec as P

MESH = pl.DeviceIdType.MESH
DK = 128
CONV = 4
HALO = 16
F32 = jnp.float32
BF16 = jnp.bfloat16


def dot(a, b):
    return jnp.dot(a, b, preferred_element_type=F32)


def dot_t(a, b):
    return lax.dot_general(a, b, (((1,), (1,)), ((), ())), preferred_element_type=F32)


def split(x):
    high = x.astype(BF16)
    return high, (x - high.astype(F32)).astype(BF16)


def mm3(a, b, product=dot):
    ah, al = split(a)
    bh, bl = split(b)
    return product(ah, bh) + (product(ah, bl) + product(al, bh))


def kernel(
    n, wins, reqs,
    lengths, qkv, conv_w, beta, out_gain, hidden, norm_gain, w_out, w_qkv,
    qkv_next, stream_out, fs_out, edge_out,
    halo, wo_own, wo_sib, wq, state_send, state_recv, nh, nh_send, nh_recv,
    part_keep, part_send, part_recv, ns, gathered, proj_send, proj_recv,
    res, up_send, up_recv, down_send, down_recv,
    local_sem, halo_sem, wo_sem, state_sem, nh_sem, part_send_sem, part_recv_sem,
    ns_send_sem, ns_recv_sem, proj_send_sem, proj_recv_sem, up_sem, down_sem,
):
    rows = qkv.shape[1]
    width = qkv.shape[2]
    heads = width // DK
    half = rows // 2
    group = wins * 2
    blk = hidden.shape[0]
    k_idx = lax.axis_index("seq")
    w = lax.axis_index("win")
    c = lax.axis_index("wout")
    me = w * 2 + c
    sib = {"wout": 1 - c}
    above = {"seq": lax.rem(k_idx + 1, n)}
    below = {"seq": lax.rem(k_idx + n - 1, n)}
    not_first = k_idx > 0
    not_last = k_idx < n - 1

    def remote(src, dst, send_sem, recv_sem, device):
        return pltpu.make_async_remote_copy(
            src_ref=src, dst_ref=dst, send_sem=send_sem, recv_sem=recv_sem,
            device_id=device, device_id_type=MESH,
        )

    def peer(o):
        p = lax.rem(me + o, group)
        return p // 2, lax.rem(p, 2)

    barrier = pltpu.get_barrier_semaphore()
    for o in range(1, group):
        pw, pc = peer(o)
        pl.semaphore_signal(barrier, inc=1, device_id={"win": pw, "wout": pc}, device_id_type=MESH)

    @pl.when(not_first)
    def _():
        pl.semaphore_signal(barrier, inc=1, device_id=below, device_id_type=MESH)

    @pl.when(not_last)
    def _():
        pl.semaphore_signal(barrier, inc=1, device_id=above, device_id_type=MESH)

    copy_wo = pltpu.make_async_copy(w_out, wo_own, local_sem.at[0])
    copy_wq = pltpu.make_async_copy(w_qkv, wq, local_sem.at[1])
    copy_wo.start()
    copy_wq.start()
    pl.semaphore_wait(
        barrier, group - 1 + not_first.astype(jnp.int32) + not_last.astype(jnp.int32)
    )

    halo_copy = remote(
        qkv.at[:, pl.ds(rows - HALO, HALO), :], halo, halo_sem.at[0], halo_sem.at[1], above
    )

    @pl.when(not_last)
    def _():
        halo_copy.start()

    wo_copy = remote(w_out, wo_sib, wo_sem.at[0], wo_sem.at[1], sib)
    wo_copy.start()

    @pl.when(jnp.logical_not(not_first))
    def _():
        halo[...] = jnp.zeros_like(halo)
        state_recv[...] = jnp.zeros_like(state_recv)

    ends = []
    total = jnp.int32(0)
    for r in range(reqs):
        total = total + lengths[r]
        ends.append(total)
    first = k_idx * rows

    def segments(positions):
        seg = jnp.zeros_like(positions)
        for r in range(reqs):
            seg = seg + (positions >= ends[r]).astype(jnp.int32)
        return jnp.where(positions < 0, -1, seg)

    def scalar_segment(position):
        seg = jnp.int32(0)
        for r in range(reqs):
            seg = seg + (position >= ends[r]).astype(jnp.int32)
        return jnp.where(position < 0, -1, seg)

    col_pos = first + lax.broadcasted_iota(jnp.int32, (rows, 1), 0)
    row_pos = first + lax.broadcasted_iota(jnp.int32, (1, rows), 1)
    col_seg = segments(col_pos)
    row_seg = segments(row_pos)
    before_seg = scalar_segment(first - 1)
    last_seg = scalar_segment(first + rows - 1)
    coupled = (col_seg == before_seg).astype(F32)
    in_last = (row_seg == last_seg).astype(F32)
    last_link = (before_seg == last_seg).astype(F32)

    ri = lax.broadcasted_iota(jnp.int32, (rows, rows), 0)
    ci = lax.broadcasted_iota(jnp.int32, (rows, rows), 1)
    same = col_seg == row_seg
    causal = same & (ri >= ci)
    strict = same & (ri > ci)
    diagonal = ri == ci
    hi_ = lax.broadcasted_iota(jnp.int32, (half, half), 0)
    hj_ = lax.broadcasted_iota(jnp.int32, (half, half), 1)
    eye_half = (hi_ == hj_).astype(F32)
    eye_keys = (
        lax.broadcasted_iota(jnp.int32, (DK, DK), 0) == lax.broadcasted_iota(jnp.int32, (DK, DK), 1)
    ).astype(F32)

    def silu(x):
        return (x / (1.0 + jnp.exp(-x))).astype(BF16).astype(F32)

    index_col = lax.broadcasted_iota(jnp.int32, (rows, 1), 0)
    keeps = [None] + [segments(col_pos - back) == col_seg for back in range(1, CONV)]

    def tap(t, back):
        return conv_w[t, CONV - 1 - back : CONV - back, :]

    pres = []
    mains = []
    for t in range(3):
        wide = qkv[t].astype(F32)
        pre = tap(t, 0) * wide
        for back in range(1, CONV):
            shifted = pltpu.roll(wide, back, axis=0)
            pre = pre + tap(t, back) * jnp.where(keeps[back] & (index_col >= back), shifted, 0.0)
        pres.append(pre[:8])
        mains.append(silu(pre)[8:])

    strength = []
    for h in range(heads):
        b_row = 1.0 / (1.0 + jnp.exp(-beta[h : h + 1, :]))
        strength.append(jnp.sum(jnp.where(diagonal, b_row, 0.0), axis=1, keepdims=True))

    @pl.when(not_first)
    def _():
        halo_copy.wait_recv()

    activated = []
    for t in range(3):
        rim = halo[t].astype(F32)[HALO - 8 :]
        pre = pres[t]
        for back in range(1, CONV):
            shifted = pltpu.roll(rim, back, axis=0)
            pre = pre + tap(t, back) * jnp.where(
                keeps[back][:8] & (index_col[:8] < back), shifted, 0.0
            )
        activated.append(jnp.concatenate([silu(pre), mains[t]], axis=0))

    def unit(x):
        return x * lax.rsqrt(jnp.sum(x * x, axis=-1, keepdims=True) + 1e-6)

    q, k, v, kt, a_full, scores = [], [], [], [], [], []
    for h in range(heads):
        cols = slice(h * DK, (h + 1) * DK)
        q.append(unit(activated[0][:, cols]))
        k.append(unit(activated[1][:, cols]))
        v.append(activated[2][:, cols])
        kt.append(jnp.transpose(k[h]))
        gram = mm3(k[h], k[h], dot_t)
        a_full.append(jnp.where(strict, strength[h] * gram, 0.0))
        scores.append(jnp.where(causal, mm3(q[h], k[h], dot_t), 0.0))

    diag = []
    for h in range(heads):
        diag.append(a_full[h][:half, :half])
        diag.append(a_full[h][half:, half:])
    level = 0
    inverse = None
    while (1 << level) < half:
        pick = (
            ((hi_ >> (level + 1)) == (hj_ >> (level + 1)))
            & (((hi_ >> level) & 1) == 1)
            & (((hj_ >> level) & 1) == 0)
        )
        lower = [jnp.where(pick, a, 0.0) for a in diag]
        if level == 0:
            inverse = [eye_half - x for x in lower]
        else:
            ys = [mm3(x, z) for x, z in zip(lower, inverse)]
            inverse = [z - mm3(z, y) for z, y in zip(inverse, ys)]
        level += 1

    solved, out_local, q_link, trans, write = [], [], [], [], []
    for h in range(heads):
        rhs = jnp.concatenate([strength[h] * v[h], (strength[h] * coupled) * k[h]], axis=1)
        top = mm3(inverse[2 * h], rhs[:half])
        low = mm3(inverse[2 * h + 1], rhs[half:] - mm3(a_full[h][half:, :half], top))
        solved.append(jnp.concatenate([top, low], axis=0))
    for h in range(heads):
        m = mm3(kt[h] * in_last, solved[h])
        write.append(m[:, :DK])
        trans.append(last_link * (eye_keys - m[:, DK:]))

    steps = n // 2
    state_copies = [
        remote(state_send.at[i], state_recv.at[i], state_sem.at[0, i], state_sem.at[1, i], above)
        for i in range(steps)
    ]
    for i in range(steps):
        if i > 0:
            pl.when(not_first)(state_copies[i - 1].wait_recv)
        for h in range(heads):
            hr = slice(h * DK, (h + 1) * DK)
            state = write[h]
            if i > 0:
                state = state + mm3(trans[h], state_recv[i - 1, hr, :].astype(F32))
            state_send[i, hr, :] = state.astype(BF16)
        pl.when(not_last)(state_copies[i].start)
        if i == 0:
            local = [mm3(scores[h], solved[h]) for h in range(heads)]
            links = [
                jnp.concatenate([coupled * q[h] - local[h][:, DK:], solved[h][:, DK:]], axis=0)
                for h in range(heads)
            ]
    pl.when(not_first)(state_copies[steps - 1].wait_recv)
    state_in = [
        state_recv[steps - 1, h * DK : (h + 1) * DK, :].astype(F32) for h in range(heads)
    ]

    corrected = []
    for h in range(heads):
        s = local[h]
        applied = mm3(links[h], state_in[h])
        att = s[:, :DK] + applied[:rows]
        corrected.append(solved[h][:, :DK] - applied[rows:])
        scale = lax.rsqrt(jnp.mean(att * att, axis=-1, keepdims=True) + 1e-5)
        nh[:, h * DK : (h + 1) * DK] = (att * scale * out_gain[...]).astype(BF16)

    for o in range(wins):
        start = pl.multiple_of((2 * o + 1 - c) * blk, blk)
        nh_send[o * blk : (o + 1) * blk, :] = nh[pl.ds(start, blk), :]
    nh_copy = remote(nh_send, nh_recv, nh_sem.at[0], nh_sem.at[1], sib)
    nh_copy.start()
    own_rows = jnp.concatenate(
        [nh[pl.ds(pl.multiple_of((2 * o + c) * blk, blk), blk), :] for o in range(wins)], axis=0
    )
    copy_wo.wait()
    wo_copy.wait_recv()
    part_keep[...] = dot(own_rows, wo_own[...])
    nh_copy.wait_recv()
    part_keep[...] = part_keep[...] + dot(nh_recv[...], wo_sib[...])
    part_copies = []
    for o in range(1, wins):
        pw = lax.rem(w + o, wins)
        part_send[o] = part_keep[pl.ds(pl.multiple_of(pw * blk, blk), blk), :].astype(BF16)
        cp = remote(
            part_send.at[o], part_recv.at[o], part_send_sem.at[o], part_recv_sem.at[o], {"win": pw}
        )
        cp.start()
        part_copies.append(cp)

    for r in range(reqs):
        owned = (ends[r] - 1 >= first) & (ends[r] - 1 < first + rows)
        owned_f = owned.astype(F32)
        member = (row_seg == r).astype(F32) * owned_f
        carry = owned_f * (before_seg == r).astype(F32)
        for h in range(heads):
            base = (r * heads + h) * DK
            res[base : base + DK, :] = (
                mm3(kt[h] * member, corrected[h]) + carry * state_in[h]
            ).astype(BF16)
    edge_base = reqs * heads * DK

    def selection(base, count):
        sel_row = lax.broadcasted_iota(jnp.int32, (16, count), 0)
        sel_pos = base + lax.broadcasted_iota(jnp.int32, (16, count), 1)
        sel_seg = segments(sel_pos)
        select = jnp.zeros((16, count), F32)
        for r in range(reqs):
            owned = (ends[r] - 1 >= first) & (ends[r] - 1 < first + rows)
            for i in range(CONV - 1):
                hit = (
                    (sel_row == r * (CONV - 1) + i)
                    & (sel_pos == ends[r] - (CONV - 1) + i)
                    & (sel_seg == r)
                )
                select = select + jnp.where(hit, 1.0, 0.0) * owned.astype(F32)
        return select.astype(BF16)

    select_halo = selection(first - HALO, HALO)
    select_own = selection(first, rows)
    pieces = width // DK
    for t in range(3):
        edge = dot(select_halo, halo[t]) + dot(select_own, qkv[t])
        for j in range(pieces):
            base = edge_base + (t * pieces + j) * 16
            res[base : base + 16, :] = edge[:, j * DK : (j + 1) * DK].astype(BF16)

    up_copy = remote(up_send, up_recv, up_sem.at[0], up_sem.at[1], above)
    down_copy = remote(down_send, down_recv, down_sem.at[0], down_sem.at[1], below)

    def up_step():
        up_copy.wait_recv()

        @pl.when(not_last)
        def _():
            up_send[...] = up_recv[...] + res[...]
            up_copy.start()

    def down_step():
        down_copy.wait_recv()

        @pl.when(not_first)
        def _():
            down_send[...] = down_recv[...] + res[...]
            down_copy.start()

    @pl.when(k_idx == 0)
    def _():
        up_recv[...] = jnp.zeros_like(up_recv)
        up_send[...] = res[...]
        up_copy.start()

    @pl.when(k_idx == n - 1)
    def _():
        down_recv[...] = jnp.zeros_like(down_recv)
        down_send[...] = res[...]
        down_copy.start()

    summed = hidden[...].astype(F32) + part_keep[pl.ds(pl.multiple_of(w * blk, blk), blk), :]
    for o in range(1, wins):
        part_copies[o - 1].wait_recv()
        summed = summed + part_recv[o].astype(F32)
    stream_out[...] = summed.astype(BF16)
    scale = lax.rsqrt(jnp.mean(summed * summed, axis=-1, keepdims=True) + 1e-5)
    ns[...] = (summed * scale * norm_gain[...]).astype(BF16)
    in_block = wq.shape[0]
    my_rows = pl.ds(pl.multiple_of(me * blk, blk), blk)
    ns_copies = []
    for o in range(1, group):
        pw, pc = peer(o)
        cp = remote(
            ns.at[:, pl.ds(pl.multiple_of(pw * in_block, in_block), in_block)],
            gathered.at[my_rows, :],
            ns_send_sem.at[o], ns_recv_sem.at[o], {"win": pw, "wout": pc},
        )
        cp.start()
        ns_copies.append(cp)
    gathered[my_rows, :] = ns[:, pl.ds(pl.multiple_of(w * in_block, in_block), in_block)]

    pl.when(k_idx == 1)(up_step)
    pl.when(k_idx == n - 2)(down_step)

    copy_wq.wait()
    for cp in ns_copies:
        cp.wait_recv()
    out_rows = blk * 2
    cols = wq.shape[1] // 2
    wy, wx = w // 2, lax.rem(w, 2)
    side, across, far = wy * 2 + (1 - wx), (1 - wy) * 2 + wx, 3 - w

    def project(pw):
        block = gathered[pl.ds(pl.multiple_of(pw * out_rows, out_rows), out_rows), :]
        return dot(block, wq[...])

    def proj_copy(i, pw):
        return remote(
            proj_send.at[i], proj_recv.at[i], proj_send_sem.at[i], proj_recv_sem.at[i], {"win": pw}
        )

    proj_copies = [proj_copy(i, pw) for i, pw in enumerate((side, across) * 2 + (across, side))]
    term = project(far).astype(BF16)
    proj_send[0] = term[:, :cols]
    proj_copies[0].start()
    proj_send[1] = term[:, cols:]
    proj_copies[1].start()
    term = project(side)
    proj_send[2] = term[:, :cols].astype(BF16)
    proj_copies[2].start()
    side_term = term[:, cols:]
    term = project(across)
    proj_send[3] = term[:, cols:].astype(BF16)
    proj_copies[3].start()
    across_term = term[:, :cols]
    own = project(w)
    proj_copies[0].wait_recv()
    proj_send[4] = (across_term + proj_recv[0].astype(F32)).astype(BF16)
    proj_copies[4].start()
    proj_copies[1].wait_recv()
    proj_send[5] = (side_term + proj_recv[1].astype(F32)).astype(BF16)
    proj_copies[5].start()

    pl.when((k_idx == 2) & (k_idx > 1))(up_step)
    pl.when((k_idx == n - 3) & (k_idx < n - 2))(down_step)
    pl.when(k_idx > 2)(up_step)
    pl.when(k_idx < n - 3)(down_step)

    total_res = res[...].astype(F32) + up_recv[...].astype(F32) + down_recv[...].astype(F32)
    fs_out[...] = total_res[:edge_base]
    for t in range(3 * pieces):
        base = edge_base + t * 16
        edge_out[:, t * DK : (t + 1) * DK] = total_res[base : base + 16]

    for cp in proj_copies[2:]:
        cp.wait_recv()
    for i, part in enumerate((slice(0, cols), slice(cols, 2 * cols))):
        qkv_next[:, part] = (
            own[:, part] + proj_recv[2 + i].astype(F32) + proj_recv[4 + i].astype(F32)
        ).astype(BF16)

    wo_copy.wait_send()
    nh_copy.wait_send()
    for cp in part_copies + ns_copies + proj_copies:
        cp.wait_send()

    @pl.when(not_last)
    def _():
        halo_copy.wait_send()
        for cp in state_copies:
            cp.wait_send()
        up_copy.wait_send()

    @pl.when(not_first)
    def _():
        down_copy.wait_send()


def place_results(
    reqs, taps, width,
    qkv_next, stream_out, states, edges,
    qkv_next_out, stream_out_out, states_out, edges_out, sems,
):
    copies = [
        pltpu.make_async_copy(src, dst, sems.at[i])
        for i, (src, dst) in enumerate(
            ((qkv_next, qkv_next_out), (stream_out, stream_out_out), (states, states_out))
        )
    ]
    for cp in copies:
        cp.start()
    for r in range(reqs):
        for i in range(taps):
            row = r * taps + i
            for t in range(3):
                edges_out[r, i, t : t + 1, :] = edges[
                    row : row + 1, t * width : (t + 1) * width
                ].astype(BF16)
    for cp in copies:
        cp.wait()


def solution(mesh):
    n, wins = mesh.shape["seq"], mesh.shape["win"]

    def body(qkv_in, conv_w, beta_logits, lengths, out_gain, w_out, hidden_in, norm_gain, w_qkv):
        rows, _, width = qkv_in.shape
        heads = width // DK
        reqs = lengths.shape[0]
        blk, model = hidden_in.shape
        in_block, out_cols = w_qkv.shape
        group = wins * 2
        res_rows = reqs * heads * DK + 16 * 3 * (width // DK)
        vmem = pl.BlockSpec(memory_space=pltpu.VMEM)
        dma = pltpu.SemaphoreType.DMA
        results = pl.pallas_call(
            functools.partial(kernel, n, wins, reqs),
            out_shape=(
                jax.ShapeDtypeStruct((blk * 2, out_cols), BF16),
                jax.ShapeDtypeStruct((blk, model), BF16),
                jax.ShapeDtypeStruct((reqs * heads * DK, DK), F32),
                jax.ShapeDtypeStruct((16, 3 * width), F32),
            ),
            in_specs=[pl.BlockSpec(memory_space=pltpu.SMEM)] + [vmem] * 6
            + [pl.BlockSpec(memory_space=pl.ANY)] * 2,
            out_specs=(vmem,) * 4,
            scratch_shapes=[
                pltpu.VMEM((3, HALO, width), BF16),
                pltpu.VMEM((width, model), BF16),
                pltpu.VMEM((width, model), BF16),
                pltpu.VMEM((in_block, out_cols), BF16),
                pltpu.VMEM((n // 2, heads * DK, DK), BF16),
                pltpu.VMEM((n // 2, heads * DK, DK), BF16),
                pltpu.VMEM((rows, width), BF16),
                pltpu.VMEM((rows // 2, width), BF16),
                pltpu.VMEM((rows // 2, width), BF16),
                pltpu.VMEM((rows // 2, model), F32),
                pltpu.VMEM((wins, blk, model), BF16),
                pltpu.VMEM((wins, blk, model), BF16),
                pltpu.VMEM((blk, model), BF16),
                pltpu.VMEM((rows, in_block), BF16),
                pltpu.VMEM((6, blk * 2, out_cols // 2), BF16),
                pltpu.VMEM((6, blk * 2, out_cols // 2), BF16),
                pltpu.VMEM((res_rows, DK), BF16),
                pltpu.VMEM((res_rows, DK), BF16),
                pltpu.VMEM((res_rows, DK), BF16),
                pltpu.VMEM((res_rows, DK), BF16),
                pltpu.VMEM((res_rows, DK), BF16),
                dma((2,)), dma((2,)), dma((2,)), dma((2, n // 2)), dma((2,)),
                dma((wins,)), dma((wins,)), dma((group,)), dma((group,)),
                dma((6,)), dma((6,)), dma((2,)), dma((2,)),
            ],
            compiler_params=pltpu.CompilerParams(
                collective_id=0, has_side_effects=True, vmem_limit_bytes=56 * 1024 * 1024
            ),
            cost_estimate=pl.CostEstimate(
                flops=4 * 10**9, bytes_accessed=8 * 10**6, transcendentals=10**6
            ),
            name="delta_sublayer",
        )(
            lengths, jnp.transpose(qkv_in, (1, 0, 2)), conv_w, beta_logits,
            out_gain.reshape(1, DK), hidden_in, norm_gain.reshape(1, model), w_out, w_qkv,
        )
        taps = CONV - 1
        place = pl.BlockSpec(memory_space=pl.ANY)
        projected, stream, states, edges = pl.pallas_call(
            functools.partial(place_results, reqs, taps, width),
            out_shape=tuple(jax.ShapeDtypeStruct(x.shape, x.dtype) for x in results[:3])
            + (jax.ShapeDtypeStruct((reqs, taps, 3, width), BF16),),
            in_specs=[place] * 3 + [vmem],
            out_specs=(place,) * 3 + (vmem,),
            scratch_shapes=[dma((3,))],
            compiler_params=pltpu.CompilerParams(vmem_limit_bytes=60 * 1024 * 1024),
            name="place_results",
        )(*results)
        return projected, stream, states.reshape(reqs, heads, DK, DK), edges

    return jax.shard_map(
        body,
        mesh=mesh,
        in_specs=(
            P("seq", None, ("win", "wout")),
            P(None, None, ("win", "wout")),
            P(("win", "wout"), "seq"),
            P(),
            P(),
            P(("win", "wout"), None),
            P(("seq", "win", "wout"), None),
            P(),
            P("win", "wout"),
        ),
        out_specs=(
            P(("seq", "win"), "wout"),
            P(("seq", "win", "wout"), None),
            P(None, ("win", "wout"), None, None),
            P(None, None, None, ("win", "wout")),
        ),
        check_vma=False,
    )
```

```python
import functools

import jax
import jax.numpy as jnp
from jax import lax
from jax.experimental import pallas as pl
from jax.experimental.pallas import tpu as pltpu
from jax.sharding import PartitionSpec as P

MESH = pl.DeviceIdType.MESH
DK = 128
CONV = 4
HALO = 16
F32 = jnp.float32
BF16 = jnp.bfloat16


def dot(a, b):
    return jnp.dot(a, b, preferred_element_type=F32)


def dot_t(a, b):
    return lax.dot_general(a, b, (((1,), (1,)), ((), ())), preferred_element_type=F32)


def split(x):
    high = x.astype(BF16)
    return high, (x - high.astype(F32)).astype(BF16)


def mm3(a, b):
    ah, al = split(a)
    bh, bl = split(b)
    return dot(ah, bh) + (dot(ah, bl) + dot(al, bh))


def mm1(a, b):
    return dot(a.astype(BF16), b.astype(BF16))


def mm_left(a, b):
    high, low = split(a)
    return dot(high, b) + dot(low, b)


def mm_right(a, b):
    high, low = split(b)
    return dot(a, high) + dot(a, low)


def kernel(
    n, wins, reqs,
    lengths, qkv, conv_w, beta, out_gain, hidden, norm_gain, w_out, w_qkv,
    qkv_next, stream_out, fs_out, edge_out,
    halo, wo_own, wo_sib, wq, state_send, state_recv, nh, nh_send, nh_recv,
    part_keep, part_send, part_recv, ns, gathered, proj_send, proj_recv,
    res, up_send, up_recv, down_send, down_recv,
    local_sem, halo_sem, wo_sem, state_sem, nh_sem, part_send_sem, part_recv_sem,
    ns_send_sem, ns_recv_sem, proj_send_sem, proj_recv_sem, up_sem, down_sem,
):
    rows = qkv.shape[1]
    width = qkv.shape[2]
    heads = width // DK
    half = rows // 2
    group = wins * 2
    blk = hidden.shape[0]
    k_idx = lax.axis_index("seq")
    w = lax.axis_index("win")
    c = lax.axis_index("wout")
    me = w * 2 + c
    sib = {"wout": 1 - c}
    above = {"seq": lax.rem(k_idx + 1, n)}
    below = {"seq": lax.rem(k_idx + n - 1, n)}
    not_first = k_idx > 0
    not_last = k_idx < n - 1

    def remote(src, dst, send_sem, recv_sem, device):
        return pltpu.make_async_remote_copy(
            src_ref=src, dst_ref=dst, send_sem=send_sem, recv_sem=recv_sem,
            device_id=device, device_id_type=MESH,
        )

    def peer(o):
        p = lax.rem(me + o, group)
        return p // 2, lax.rem(p, 2)

    barrier = pltpu.get_barrier_semaphore()
    for o in range(1, group):
        pw, pc = peer(o)
        pl.semaphore_signal(barrier, inc=1, device_id={"win": pw, "wout": pc}, device_id_type=MESH)

    @pl.when(not_first)
    def _():
        pl.semaphore_signal(barrier, inc=1, device_id=below, device_id_type=MESH)

    @pl.when(not_last)
    def _():
        pl.semaphore_signal(barrier, inc=1, device_id=above, device_id_type=MESH)

    copy_wo = pltpu.make_async_copy(w_out, wo_own, local_sem.at[0])
    copy_wq = pltpu.make_async_copy(w_qkv, wq, local_sem.at[1])
    copy_wo.start()
    copy_wq.start()
    pl.semaphore_wait(
        barrier, group - 1 + not_first.astype(jnp.int32) + not_last.astype(jnp.int32)
    )

    halo_copy = remote(
        qkv.at[:, pl.ds(rows - HALO, HALO), :], halo, halo_sem.at[0], halo_sem.at[1], above
    )

    @pl.when(not_last)
    def _():
        halo_copy.start()

    wo_copy = remote(w_out, wo_sib, wo_sem.at[0], wo_sem.at[1], sib)
    wo_copy.start()

    @pl.when(jnp.logical_not(not_first))
    def _():
        halo[...] = jnp.zeros_like(halo)
        state_recv[...] = jnp.zeros_like(state_recv)

    ends = []
    total = jnp.int32(0)
    for r in range(reqs):
        total = total + lengths[r]
        ends.append(total)
    first = k_idx * rows

    def segments(positions):
        seg = jnp.zeros_like(positions)
        for r in range(reqs):
            seg = seg + (positions >= ends[r]).astype(jnp.int32)
        return jnp.where(positions < 0, -1, seg)

    def scalar_segment(position):
        seg = jnp.int32(0)
        for r in range(reqs):
            seg = seg + (position >= ends[r]).astype(jnp.int32)
        return jnp.where(position < 0, -1, seg)

    col_pos = first + lax.broadcasted_iota(jnp.int32, (rows, 1), 0)
    row_pos = first + lax.broadcasted_iota(jnp.int32, (1, rows), 1)
    col_seg = segments(col_pos)
    row_seg = segments(row_pos)
    before_seg = scalar_segment(first - 1)
    last_seg = scalar_segment(first + rows - 1)
    coupled = (col_seg == before_seg).astype(F32)
    in_last = (row_seg == last_seg).astype(F32)
    last_link = (before_seg == last_seg).astype(F32)

    ri = lax.broadcasted_iota(jnp.int32, (rows, rows), 0)
    ci = lax.broadcasted_iota(jnp.int32, (rows, rows), 1)
    same = col_seg == row_seg
    causal = same & (ri >= ci)
    strict = same & (ri > ci)
    diagonal = ri == ci
    hi_ = lax.broadcasted_iota(jnp.int32, (half, half), 0)
    hj_ = lax.broadcasted_iota(jnp.int32, (half, half), 1)
    eye_half = (hi_ == hj_).astype(F32)
    eye_keys = (
        lax.broadcasted_iota(jnp.int32, (DK, DK), 0) == lax.broadcasted_iota(jnp.int32, (DK, DK), 1)
    ).astype(F32)

    def silu(x):
        return (x / (1.0 + jnp.exp(-x))).astype(BF16).astype(F32)

    index_col = lax.broadcasted_iota(jnp.int32, (rows, 1), 0)
    keeps = [None] + [segments(col_pos - back) == col_seg for back in range(1, CONV)]

    def tap(t, back):
        return conv_w[t, CONV - 1 - back : CONV - back, :]

    pres = []
    mains = []
    for t in range(3):
        wide = qkv[t].astype(F32)
        pre = tap(t, 0) * wide
        for back in range(1, CONV):
            shifted = pltpu.roll(wide, back, axis=0)
            pre = pre + tap(t, back) * jnp.where(keeps[back] & (index_col >= back), shifted, 0.0)
        pres.append(pre[:8])
        mains.append(silu(pre)[8:])

    strength = []
    for h in range(heads):
        b_row = 1.0 / (1.0 + jnp.exp(-beta[h : h + 1, :]))
        strength.append(jnp.sum(jnp.where(diagonal, b_row, 0.0), axis=1, keepdims=True))

    @pl.when(not_first)
    def _():
        halo_copy.wait_recv()

    activated = []
    for t in range(3):
        rim = halo[t].astype(F32)[HALO - 8 :]
        pre = pres[t]
        for back in range(1, CONV):
            shifted = pltpu.roll(rim, back, axis=0)
            pre = pre + tap(t, back) * jnp.where(
                keeps[back][:8] & (index_col[:8] < back), shifted, 0.0
            )
        activated.append(jnp.concatenate([silu(pre), mains[t]], axis=0))

    def norm_factor(x, axis):
        return lax.rsqrt(jnp.sum(x * x, axis=axis, keepdims=True) + 1e-6)

    q, k, v, kt, k_col, a_full, scores = [], [], [], [], [], [], []
    for h in range(heads):
        cols = slice(h * DK, (h + 1) * DK)
        q_raw, k_raw = activated[0][:, cols], activated[1][:, cols]
        q_col = norm_factor(q_raw, 1)
        k_col.append(norm_factor(k_raw, 1))
        kt_raw = jnp.transpose(k_raw)
        k_row = norm_factor(kt_raw, 0)
        q.append(q_raw * q_col)
        k.append(k_raw * k_col[h])
        v.append(activated[2][:, cols])
        kt.append(kt_raw)
        k_half = k_raw.astype(BF16)
        gram = dot_t(k_half, k_half) * k_row
        a_full.append(jnp.where(strict, (strength[h] * k_col[h]) * gram, 0.0))
        scores.append(
            jnp.where(causal, q_col * (dot_t(q_raw.astype(BF16), k_half) * k_row), 0.0)
        )

    diag = []
    for h in range(heads):
        diag.append(a_full[h][:half, :half])
        diag.append(a_full[h][half:, half:])
    level = 0
    inverse = None
    while (1 << level) < half:
        pick = (
            ((hi_ >> (level + 1)) == (hj_ >> (level + 1)))
            & (((hi_ >> level) & 1) == 1)
            & (((hj_ >> level) & 1) == 0)
        )
        lower = [jnp.where(pick, a, 0.0) for a in diag]
        if level == 0:
            inverse = [eye_half - x for x in lower]
        else:
            ys = [mm1(x, z) for x, z in zip(lower, inverse)]
            inverse = [z - mm1(z, y) for z, y in zip(inverse, ys)]
        level += 1

    solved, out_local, q_link, trans, write = [], [], [], [], []
    for h in range(heads):
        rhs = jnp.concatenate([strength[h] * v[h], (strength[h] * coupled) * k[h]], axis=1)
        top = mm3(inverse[2 * h], rhs[:half])
        low = mm3(inverse[2 * h + 1], rhs[half:] - mm1(a_full[h][half:, :half], top))
        solved.append(jnp.concatenate([top, low], axis=0))
    for h in range(heads):
        m = mm_right((kt[h] * in_last).astype(BF16), k_col[h] * solved[h])
        write.append(m[:, :DK])
        trans.append(last_link * (eye_keys - m[:, DK:]))

    steps = n // 2
    state_copies = [
        remote(state_send.at[i], state_recv.at[i], state_sem.at[0, i], state_sem.at[1, i], above)
        for i in range(steps)
    ]
    for i in range(steps):
        if i > 0:
            pl.when(not_first)(state_copies[i - 1].wait_recv)
        for h in range(heads):
            hr = slice(h * DK, (h + 1) * DK)
            state = write[h]
            if i > 0:
                state = state + mm_left(trans[h], state_recv[i - 1, hr, :])
            state_send[i, hr, :] = state.astype(BF16)
        pl.when(not_last)(state_copies[i].start)
        if i == 0:
            local = [mm1(scores[h], solved[h]) for h in range(heads)]
            links = [coupled * q[h] - local[h][:, DK:] for h in range(heads)]
    pl.when(not_first)(state_copies[steps - 1].wait_recv)
    state_in = [
        state_recv[steps - 1, h * DK : (h + 1) * DK, :] for h in range(heads)
    ]

    corrected = []
    for h in range(heads):
        att = local[h][:, :DK] + dot(links[h].astype(BF16), state_in[h])
        corrected.append(k_col[h] * (solved[h][:, :DK] - mm_left(solved[h][:, DK:], state_in[h])))
        scale = lax.rsqrt(jnp.mean(att * att, axis=-1, keepdims=True) + 1e-5)
        nh[:, h * DK : (h + 1) * DK] = (att * scale * out_gain[...]).astype(BF16)

    wy, wx = w // 2, lax.rem(w, 2)
    side, across, far = wy * 2 + (1 - wx), (1 - wy) * 2 + wx, 3 - w
    order = (w, side, across, far)

    def rows_for(pw, pc):
        return nh[pl.ds(pl.multiple_of((2 * pw + pc) * blk, blk), blk), :]

    for i, pw in enumerate(order):
        nh_send[i * blk : (i + 1) * blk, :] = rows_for(pw, 1 - c)
    nh_copy = remote(nh_send, nh_recv, nh_sem.at[0], nh_sem.at[1], sib)
    nh_copy.start()

    for r in range(reqs):
        owned = (ends[r] - 1 >= first) & (ends[r] - 1 < first + rows)
        owned_f = owned.astype(F32)
        member = (row_seg == r).astype(F32) * owned_f
        carry = owned_f * (before_seg == r).astype(F32)
        for h in range(heads):
            base = (r * heads + h) * DK
            res[base : base + DK, :] = (
                mm_right((kt[h] * member).astype(BF16), corrected[h])
                + carry * state_in[h].astype(F32)
            ).astype(BF16)
    edge_base = reqs * heads * DK

    def selection(base, count):
        sel_row = lax.broadcasted_iota(jnp.int32, (16, count), 0)
        sel_pos = base + lax.broadcasted_iota(jnp.int32, (16, count), 1)
        sel_seg = segments(sel_pos)
        select = jnp.zeros((16, count), F32)
        for r in range(reqs):
            owned = (ends[r] - 1 >= first) & (ends[r] - 1 < first + rows)
            for i in range(CONV - 1):
                hit = (
                    (sel_row == r * (CONV - 1) + i)
                    & (sel_pos == ends[r] - (CONV - 1) + i)
                    & (sel_seg == r)
                )
                select = select + jnp.where(hit, 1.0, 0.0) * owned.astype(F32)
        return select.astype(BF16)

    select_halo = selection(first - HALO, HALO)
    select_own = selection(first, rows)
    pieces = width // DK
    for t in range(3):
        edge = dot(select_halo, halo[t]) + dot(select_own, qkv[t])
        for j in range(pieces):
            base = edge_base + (t * pieces + j) * 16
            res[base : base + 16, :] = edge[:, j * DK : (j + 1) * DK].astype(BF16)

    up_copy = remote(up_send, up_recv, up_sem.at[0], up_sem.at[1], above)
    down_copy = remote(down_send, down_recv, down_sem.at[0], down_sem.at[1], below)

    def up_step():
        up_copy.wait_recv()

        @pl.when(not_last)
        def _():
            up_send[...] = up_recv[...] + res[...]
            up_copy.start()

    def down_step():
        down_copy.wait_recv()

        @pl.when(not_first)
        def _():
            down_send[...] = down_recv[...] + res[...]
            down_copy.start()

    @pl.when(k_idx == 0)
    def _():
        up_recv[...] = jnp.zeros_like(up_recv)
        up_send[...] = res[...]
        up_copy.start()

    @pl.when(k_idx == n - 1)
    def _():
        down_recv[...] = jnp.zeros_like(down_recv)
        down_send[...] = res[...]
        down_copy.start()

    own_rows = jnp.concatenate([rows_for(pw, c) for pw in order], axis=0)
    copy_wo.wait()
    part_keep[...] = dot(own_rows, wo_own[...])
    wo_copy.wait_recv()
    nh_copy.wait_recv()

    def win_copies(send, recv, send_sem, recv_sem):
        return [
            remote(send.at[i], recv.at[i], send_sem.at[i], recv_sem.at[i], {"win": pw})
            for i, pw in enumerate((side, across) * 2 + (across, side))
        ]

    part_copies = win_copies(part_send, part_recv, part_send_sem, part_recv_sem)
    model = hidden.shape[1]
    part_cols = model // 2

    def relay(copies, send, recv, cols, far_term, side_term, across_term, own_term):
        term = far_term().astype(BF16)
        send[0] = term[:, :cols]
        copies[0].start()
        send[1] = term[:, cols:]
        copies[1].start()
        term = side_term()
        send[2] = term[:, :cols].astype(BF16)
        copies[2].start()
        side_rest = term[:, cols:]
        term = across_term()
        send[3] = term[:, cols:].astype(BF16)
        copies[3].start()
        across_rest = term[:, :cols]
        own = own_term()
        copies[0].wait_recv()
        send[4] = (across_rest + recv[0].astype(F32)).astype(BF16)
        copies[4].start()
        copies[1].wait_recv()
        send[5] = (side_rest + recv[1].astype(F32)).astype(BF16)
        copies[5].start()
        return own

    part_all = part_keep[...] + dot(nh_recv[...], wo_sib[...])
    part_terms = [part_all[i * blk : (i + 1) * blk] for i in range(wins)]
    own_part = relay(
        part_copies, part_send, part_recv, part_cols,
        lambda: part_terms[3], lambda: part_terms[1], lambda: part_terms[2],
        lambda: part_terms[0] + hidden[...].astype(F32),
    )

    for cp in part_copies[2:]:
        cp.wait_recv()
    summed = own_part + jnp.concatenate(
        [part_recv[2 + i].astype(F32) + part_recv[4 + i].astype(F32) for i in range(2)], axis=1
    )
    stream_out[...] = summed.astype(BF16)
    scale = lax.rsqrt(jnp.mean(summed * summed, axis=-1, keepdims=True) + 1e-5)
    ns[...] = (summed * scale * norm_gain[...]).astype(BF16)
    in_block = wq.shape[0]
    my_rows = pl.ds(pl.multiple_of(me * blk, blk), blk)
    ns_copies = []
    for o in range(1, group):
        pw, pc = peer(o)
        cp = remote(
            ns.at[:, pl.ds(pl.multiple_of(pw * in_block, in_block), in_block)],
            gathered.at[my_rows, :],
            ns_send_sem.at[o], ns_recv_sem.at[o], {"win": pw, "wout": pc},
        )
        cp.start()
        ns_copies.append(cp)
    gathered[my_rows, :] = ns[:, pl.ds(pl.multiple_of(w * in_block, in_block), in_block)]

    pl.when(k_idx == 1)(up_step)
    pl.when(k_idx == n - 2)(down_step)

    copy_wq.wait()
    for cp in ns_copies:
        cp.wait_recv()
    out_rows = blk * 2
    cols = wq.shape[1] // 2

    def project(pw):
        block = gathered[pl.ds(pl.multiple_of(pw * out_rows, out_rows), out_rows), :]
        return dot(block, wq[...])

    proj_copies = win_copies(proj_send, proj_recv, proj_send_sem, proj_recv_sem)
    own = relay(
        proj_copies, proj_send, proj_recv, cols,
        lambda: project(far), lambda: project(side), lambda: project(across), lambda: project(w),
    )

    pl.when((k_idx == 2) & (k_idx > 1))(up_step)
    pl.when((k_idx == n - 3) & (k_idx < n - 2))(down_step)
    pl.when(k_idx > 2)(up_step)
    pl.when(k_idx < n - 3)(down_step)

    total_res = res[...].astype(F32) + up_recv[...].astype(F32) + down_recv[...].astype(F32)
    fs_out[...] = total_res[:edge_base]
    for t in range(3 * pieces):
        base = edge_base + t * 16
        edge_out[:, t * DK : (t + 1) * DK] = total_res[base : base + 16]

    for cp in proj_copies[2:]:
        cp.wait_recv()
    for i, part in enumerate((slice(0, cols), slice(cols, 2 * cols))):
        qkv_next[:, part] = (
            own[:, part] + proj_recv[2 + i].astype(F32) + proj_recv[4 + i].astype(F32)
        ).astype(BF16)

    wo_copy.wait_send()
    nh_copy.wait_send()
    for cp in part_copies + ns_copies + proj_copies:
        cp.wait_send()

    @pl.when(not_last)
    def _():
        halo_copy.wait_send()
        for cp in state_copies:
            cp.wait_send()
        up_copy.wait_send()

    @pl.when(not_first)
    def _():
        down_copy.wait_send()


def place_results(
    reqs, taps, width,
    qkv_next, stream_out, states, edges,
    qkv_next_out, stream_out_out, states_out, edges_out,
    qkv_held, stream_held, states_held, edges_held, sems,
):
    held = (qkv_held, stream_held, states_held)
    arrive = [
        pltpu.make_async_copy(src, dst, sems.at[i])
        for i, (src, dst) in enumerate(zip((qkv_next, stream_out, states), held))
    ]
    leave = [
        pltpu.make_async_copy(src, dst, sems.at[3 + i])
        for i, (src, dst) in enumerate(
            zip(held + (edges_held,), (qkv_next_out, stream_out_out, states_out, edges_out))
        )
    ]
    for cp in arrive:
        cp.start()
    for r in range(reqs):
        for i in range(taps):
            row = r * taps + i
            for t in range(3):
                edges_held[r, i, t : t + 1, :] = edges[
                    row : row + 1, t * width : (t + 1) * width
                ].astype(BF16)
    leave[3].start()
    for i in range(3):
        arrive[i].wait()
        leave[i].start()
    for cp in leave:
        cp.wait()


def solution(mesh):
    n, wins = mesh.shape["seq"], mesh.shape["win"]

    def body(qkv_in, conv_w, beta_logits, lengths, out_gain, w_out, hidden_in, norm_gain, w_qkv):
        rows, _, width = qkv_in.shape
        heads = width // DK
        reqs = lengths.shape[0]
        blk, model = hidden_in.shape
        in_block, out_cols = w_qkv.shape
        group = wins * 2
        res_rows = reqs * heads * DK + 16 * 3 * (width // DK)
        vmem = pl.BlockSpec(memory_space=pltpu.VMEM)
        dma = pltpu.SemaphoreType.DMA
        results = pl.pallas_call(
            functools.partial(kernel, n, wins, reqs),
            out_shape=(
                jax.ShapeDtypeStruct((blk * 2, out_cols), BF16),
                jax.ShapeDtypeStruct((blk, model), BF16),
                jax.ShapeDtypeStruct((reqs * heads * DK, DK), F32),
                jax.ShapeDtypeStruct((16, 3 * width), F32),
            ),
            in_specs=[pl.BlockSpec(memory_space=pltpu.SMEM)] + [vmem] * 6
            + [pl.BlockSpec(memory_space=pl.ANY)] * 2,
            out_specs=(vmem,) * 4,
            scratch_shapes=[
                pltpu.VMEM((3, HALO, width), BF16),
                pltpu.VMEM((width, model), BF16),
                pltpu.VMEM((width, model), BF16),
                pltpu.VMEM((in_block, out_cols), BF16),
                pltpu.VMEM((n // 2, heads * DK, DK), BF16),
                pltpu.VMEM((n // 2, heads * DK, DK), BF16),
                pltpu.VMEM((rows, width), BF16),
                pltpu.VMEM((rows // 2, width), BF16),
                pltpu.VMEM((rows // 2, width), BF16),
                pltpu.VMEM((rows // 2, model), F32),
                pltpu.VMEM((6, blk, model // 2), BF16),
                pltpu.VMEM((6, blk, model // 2), BF16),
                pltpu.VMEM((blk, model), BF16),
                pltpu.VMEM((rows, in_block), BF16),
                pltpu.VMEM((6, blk * 2, out_cols // 2), BF16),
                pltpu.VMEM((6, blk * 2, out_cols // 2), BF16),
                pltpu.VMEM((res_rows, DK), BF16),
                pltpu.VMEM((res_rows, DK), BF16),
                pltpu.VMEM((res_rows, DK), BF16),
                pltpu.VMEM((res_rows, DK), BF16),
                pltpu.VMEM((res_rows, DK), BF16),
                dma((2,)), dma((2,)), dma((2,)), dma((2, n // 2)), dma((2,)),
                dma((6,)), dma((6,)), dma((group,)), dma((group,)),
                dma((6,)), dma((6,)), dma((2,)), dma((2,)),
            ],
            compiler_params=pltpu.CompilerParams(
                collective_id=0, has_side_effects=True, vmem_limit_bytes=56 * 1024 * 1024
            ),
            cost_estimate=pl.CostEstimate(
                flops=4 * 10**9, bytes_accessed=8 * 10**6, transcendentals=10**6
            ),
            name="delta_sublayer",
        )(
            lengths, jnp.transpose(qkv_in, (1, 0, 2)), conv_w, beta_logits,
            out_gain.reshape(1, DK), hidden_in, norm_gain.reshape(1, model), w_out, w_qkv,
        )
        taps = CONV - 1
        place = pl.BlockSpec(memory_space=pl.ANY)
        projected, stream, states, edges = pl.pallas_call(
            functools.partial(place_results, reqs, taps, width),
            out_shape=tuple(jax.ShapeDtypeStruct(x.shape, x.dtype) for x in results[:3])
            + (jax.ShapeDtypeStruct((reqs, taps, 3, width), BF16),),
            in_specs=[place] * 3 + [vmem],
            out_specs=(place,) * 4,
            scratch_shapes=[pltpu.VMEM(x.shape, x.dtype) for x in results[:3]]
            + [pltpu.VMEM((reqs, taps, 3, width), BF16), dma((7,))],
            compiler_params=pltpu.CompilerParams(vmem_limit_bytes=60 * 1024 * 1024),
            name="place_results",
        )(*results)
        return projected, stream, states.reshape(reqs, heads, DK, DK), edges

    return jax.shard_map(
        body,
        mesh=mesh,
        in_specs=(
            P("seq", None, ("win", "wout")),
            P(None, None, ("win", "wout")),
            P(("win", "wout"), "seq"),
            P(),
            P(),
            P(("win", "wout"), None),
            P(("seq", "win", "wout"), None),
            P(),
            P("win", "wout"),
        ),
        out_specs=(
            P(("seq", "win"), "wout"),
            P(("seq", "win", "wout"), None),
            P(None, ("win", "wout"), None, None),
            P(None, None, None, ("win", "wout")),
        ),
        check_vma=False,
    )
```

```python
import functools

import jax
import jax.numpy as jnp
from jax import lax
from jax.experimental import pallas as pl
from jax.experimental.pallas import tpu as pltpu
from jax.sharding import PartitionSpec as P

MESH = pl.DeviceIdType.MESH
DK = 128
CONV = 4
HALO = 16
F32 = jnp.float32
BF16 = jnp.bfloat16


def dot(a, b):
    return jnp.dot(a, b, preferred_element_type=F32)


def dot_t(a, b):
    return lax.dot_general(a, b, (((1,), (1,)), ((), ())), preferred_element_type=F32)


def split(x):
    high = x.astype(BF16)
    return high, (x - high.astype(F32)).astype(BF16)


def mm3(a, b):
    ah, al = split(a)
    bh, bl = split(b)
    return dot(ah, bh) + (dot(ah, bl) + dot(al, bh))


def mm1(a, b):
    return dot(a.astype(BF16), b.astype(BF16))


def mm_left(a, b):
    high, low = split(a)
    return dot(high, b) + dot(low, b)


def mm_right(a, b):
    high, low = split(b)
    return dot(a, high) + dot(a, low)


def kernel(
    n, wins, reqs,
    lengths, qkv, conv_w, beta, out_gain, hidden, norm_gain, w_out, w_qkv,
    qkv_next, stream_hbm, fs_hbm, edge_out,
    stream_out, fs_out, halo, wo_own, wo_sib, wq, state_send, state_recv, nh, nh_send, nh_recv,
    part_keep, part_send, part_recv, ns, gathered, proj_send, proj_recv,
    res, up_send, up_recv, down_send, down_recv,
    local_sem, halo_sem, wo_sem, state_sem, nh_sem, part_send_sem, part_recv_sem,
    ns_send_sem, ns_recv_sem, proj_send_sem, proj_recv_sem, up_sem, down_sem,
):
    rows = qkv.shape[1]
    width = qkv.shape[2]
    heads = width // DK
    half = rows // 2
    group = wins * 2
    blk = hidden.shape[0]
    k_idx = lax.axis_index("seq")
    w = lax.axis_index("win")
    c = lax.axis_index("wout")
    me = w * 2 + c
    sib = {"wout": 1 - c}
    above = {"seq": lax.rem(k_idx + 1, n)}
    below = {"seq": lax.rem(k_idx + n - 1, n)}
    not_first = k_idx > 0
    not_last = k_idx < n - 1

    def remote(src, dst, send_sem, recv_sem, device):
        return pltpu.make_async_remote_copy(
            src_ref=src, dst_ref=dst, send_sem=send_sem, recv_sem=recv_sem,
            device_id=device, device_id_type=MESH,
        )

    def peer(o):
        p = lax.rem(me + o, group)
        return p // 2, lax.rem(p, 2)

    barrier = pltpu.get_barrier_semaphore()
    for o in range(1, group):
        pw, pc = peer(o)
        pl.semaphore_signal(barrier, inc=1, device_id={"win": pw, "wout": pc}, device_id_type=MESH)

    @pl.when(not_first)
    def _():
        pl.semaphore_signal(barrier, inc=1, device_id=below, device_id_type=MESH)

    @pl.when(not_last)
    def _():
        pl.semaphore_signal(barrier, inc=1, device_id=above, device_id_type=MESH)

    copy_wo = pltpu.make_async_copy(w_out, wo_own, local_sem.at[0])
    copy_wq = pltpu.make_async_copy(w_qkv, wq, local_sem.at[1])
    copy_wo.start()
    copy_wq.start()
    ends = []
    total = jnp.int32(0)
    for r in range(reqs):
        total = total + lengths[r]
        ends.append(total)
    first = k_idx * rows

    def segments(positions):
        seg = jnp.zeros_like(positions)
        for r in range(reqs):
            seg = seg + (positions >= ends[r]).astype(jnp.int32)
        return jnp.where(positions < 0, -1, seg)

    def scalar_segment(position):
        seg = jnp.int32(0)
        for r in range(reqs):
            seg = seg + (position >= ends[r]).astype(jnp.int32)
        return jnp.where(position < 0, -1, seg)

    col_pos = first + lax.broadcasted_iota(jnp.int32, (rows, 1), 0)
    row_pos = first + lax.broadcasted_iota(jnp.int32, (1, rows), 1)
    col_seg = segments(col_pos)
    row_seg = segments(row_pos)
    before_seg = scalar_segment(first - 1)
    last_seg = scalar_segment(first + rows - 1)
    coupled = (col_seg == before_seg).astype(F32)
    in_last = (row_seg == last_seg).astype(F32)
    last_link = (before_seg == last_seg).astype(F32)

    ri = lax.broadcasted_iota(jnp.int32, (rows, rows), 0)
    ci = lax.broadcasted_iota(jnp.int32, (rows, rows), 1)
    same = col_seg == row_seg
    causal = same & (ri >= ci)
    strict = same & (ri > ci)
    diagonal = ri == ci
    hi_ = lax.broadcasted_iota(jnp.int32, (half, half), 0)
    hj_ = lax.broadcasted_iota(jnp.int32, (half, half), 1)
    eye_half = (hi_ == hj_).astype(F32)
    eye_keys = (
        lax.broadcasted_iota(jnp.int32, (DK, DK), 0) == lax.broadcasted_iota(jnp.int32, (DK, DK), 1)
    ).astype(F32)

    def silu(x):
        return (x / (1.0 + jnp.exp(-x))).astype(BF16).astype(F32)

    index_col = lax.broadcasted_iota(jnp.int32, (rows, 1), 0)
    keeps = [None] + [segments(col_pos - back) == col_seg for back in range(1, CONV)]

    def tap(t, back):
        return conv_w[t, CONV - 1 - back : CONV - back, :]

    pres = []
    mains = []
    def convolve(t):
        wide = qkv[t].astype(F32)
        pre = tap(t, 0) * wide
        for back in range(1, CONV):
            shifted = pltpu.roll(wide, back, axis=0)
            pre = pre + tap(t, back) * jnp.where(keeps[back] & (index_col >= back), shifted, 0.0)
        pres.append(pre[:8])
        mains.append(silu(pre)[8:])

    convolve(0)
    pl.semaphore_wait(
        barrier, group - 1 + not_first.astype(jnp.int32) + not_last.astype(jnp.int32)
    )

    halo_copy = remote(
        qkv.at[:, pl.ds(rows - HALO, HALO), :], halo, halo_sem.at[0], halo_sem.at[1], above
    )

    @pl.when(not_last)
    def _():
        halo_copy.start()

    wo_copy = remote(w_out, wo_sib, wo_sem.at[0], wo_sem.at[1], sib)
    wo_copy.start()

    @pl.when(jnp.logical_not(not_first))
    def _():
        halo[...] = jnp.zeros_like(halo)
        state_recv[...] = jnp.zeros_like(state_recv)

    convolve(1)
    convolve(2)
    strength = []
    for h in range(heads):
        b_row = 1.0 / (1.0 + jnp.exp(-beta[h : h + 1, :]))
        strength.append(jnp.sum(jnp.where(diagonal, b_row, 0.0), axis=1, keepdims=True))

    @pl.when(not_first)
    def _():
        halo_copy.wait_recv()

    activated = []
    for t in range(3):
        rim = halo[t].astype(F32)[HALO - 8 :]
        pre = pres[t]
        for back in range(1, CONV):
            shifted = pltpu.roll(rim, back, axis=0)
            pre = pre + tap(t, back) * jnp.where(
                keeps[back][:8] & (index_col[:8] < back), shifted, 0.0
            )
        activated.append(jnp.concatenate([silu(pre), mains[t]], axis=0))

    def norm_factor(x, axis):
        return lax.rsqrt(jnp.sum(x * x, axis=axis, keepdims=True) + 1e-6)

    q, k, v, kt, k_col, a_full, scores = [], [], [], [], [], [], []
    for h in range(heads):
        cols = slice(h * DK, (h + 1) * DK)
        q_raw, k_raw = activated[0][:, cols], activated[1][:, cols]
        q_col = norm_factor(q_raw, 1)
        k_col.append(norm_factor(k_raw, 1))
        kt_raw = jnp.transpose(k_raw)
        k_row = norm_factor(kt_raw, 0)
        q.append(q_raw * q_col)
        k.append(k_raw * k_col[h])
        v.append(activated[2][:, cols])
        kt.append(kt_raw)
        k_half = k_raw.astype(BF16)
        gram = dot_t(k_half, k_half) * k_row
        a_full.append(jnp.where(strict, (strength[h] * k_col[h]) * gram, 0.0))
        scores.append(
            jnp.where(causal, q_col * (dot_t(q_raw.astype(BF16), k_half) * k_row), 0.0)
        )

    diag = []
    for h in range(heads):
        diag.append(a_full[h][:half, :half])
        diag.append(a_full[h][half:, half:])
    level = 0
    inverse = None
    while (1 << level) < half:
        pick = (
            ((hi_ >> (level + 1)) == (hj_ >> (level + 1)))
            & (((hi_ >> level) & 1) == 1)
            & (((hj_ >> level) & 1) == 0)
        )
        lower = [jnp.where(pick, a, 0.0) for a in diag]
        if level == 0:
            inverse = [eye_half - x for x in lower]
        else:
            ys = [mm1(x, z) for x, z in zip(lower, inverse)]
            inverse = [z - mm1(z, y) for z, y in zip(inverse, ys)]
        level += 1

    solved, out_local, q_link, trans, write = [], [], [], [], []
    for h in range(heads):
        rhs = jnp.concatenate([strength[h] * v[h], (strength[h] * coupled) * k[h]], axis=1)
        top = mm3(inverse[2 * h], rhs[:half])
        low = mm3(inverse[2 * h + 1], rhs[half:] - mm1(a_full[h][half:, :half], top))
        solved.append(jnp.concatenate([top, low], axis=0))
    for h in range(heads):
        m = mm_right((kt[h] * in_last).astype(BF16), k_col[h] * solved[h])
        write.append(m[:, :DK])
        trans.append(last_link * (eye_keys - m[:, DK:]))

    steps = n // 2
    state_copies = [
        [
            remote(
                state_send.at[i, pl.ds(h * DK, DK)], state_recv.at[i, pl.ds(h * DK, DK)],
                state_sem.at[0, i * heads + h], state_sem.at[1, i * heads + h], above,
            )
            for h in range(heads)
        ]
        for i in range(steps)
    ]
    for i in range(steps):
        for h in range(heads):
            hr = slice(h * DK, (h + 1) * DK)
            state = write[h]
            if i > 0:
                pl.when(not_first)(state_copies[i - 1][h].wait_recv)
                state = state + mm_left(trans[h], state_recv[i - 1, hr, :])
            state_send[i, hr, :] = state.astype(BF16)
            pl.when(not_last)(state_copies[i][h].start)
        if i == 0:
            local = [mm1(scores[h], solved[h]) for h in range(heads)]
            links = [coupled * q[h] - local[h][:, DK:] for h in range(heads)]
    state_in = []

    corrected = []
    for h in range(heads):
        pl.when(not_first)(state_copies[steps - 1][h].wait_recv)
        state_in.append(state_recv[steps - 1, h * DK : (h + 1) * DK, :])
        att = local[h][:, :DK] + dot(links[h].astype(BF16), state_in[h])
        corrected.append(k_col[h] * (solved[h][:, :DK] - mm_left(solved[h][:, DK:], state_in[h])))
        scale = lax.rsqrt(jnp.mean(att * att, axis=-1, keepdims=True) + 1e-5)
        nh[:, h * DK : (h + 1) * DK] = (att * scale * out_gain[...]).astype(BF16)

    wy, wx = w // 2, lax.rem(w, 2)
    side, across, far = wy * 2 + (1 - wx), (1 - wy) * 2 + wx, 3 - w
    order = (w, side, across, far)

    def rows_for(pw, pc):
        return nh[pl.ds(pl.multiple_of((2 * pw + pc) * blk, blk), blk), :]

    for i, pw in enumerate(order):
        nh_send[i * blk : (i + 1) * blk, :] = rows_for(pw, 1 - c)
    nh_copy = remote(nh_send, nh_recv, nh_sem.at[0], nh_sem.at[1], sib)
    nh_copy.start()

    for r in range(reqs):
        owned = (ends[r] - 1 >= first) & (ends[r] - 1 < first + rows)
        owned_f = owned.astype(F32)
        member = (row_seg == r).astype(F32) * owned_f
        carry = owned_f * (before_seg == r).astype(F32)
        for h in range(heads):
            base = (r * heads + h) * DK
            res[base : base + DK, :] = (
                mm_right((kt[h] * member).astype(BF16), corrected[h])
                + carry * state_in[h].astype(F32)
            ).astype(BF16)
    edge_base = reqs * heads * DK

    def selection(base, count):
        sel_row = lax.broadcasted_iota(jnp.int32, (16, count), 0)
        sel_pos = base + lax.broadcasted_iota(jnp.int32, (16, count), 1)
        sel_seg = segments(sel_pos)
        select = jnp.zeros((16, count), F32)
        for r in range(reqs):
            owned = (ends[r] - 1 >= first) & (ends[r] - 1 < first + rows)
            for i in range(CONV - 1):
                hit = (
                    (sel_row == i * reqs + r)
                    & (sel_pos == ends[r] - (CONV - 1) + i)
                    & (sel_seg == r)
                )
                select = select + jnp.where(hit, 1.0, 0.0) * owned.astype(F32)
        return select.astype(BF16)

    select_halo = selection(first - HALO, HALO)
    select_own = selection(first, rows)
    pieces = width // DK
    for t in range(3):
        edge = dot(select_halo, halo[t]) + dot(select_own, qkv[t])
        for j in range(pieces):
            base = edge_base + (t * pieces + j) * 16
            res[base : base + 16, :] = edge[:, j * DK : (j + 1) * DK].astype(BF16)

    up_copy = remote(up_send, up_recv, up_sem.at[0], up_sem.at[1], above)
    down_copy = remote(down_send, down_recv, down_sem.at[0], down_sem.at[1], below)

    def up_step():
        up_copy.wait_recv()

        @pl.when(not_last)
        def _():
            up_send[...] = up_recv[...] + res[...]
            up_copy.start()

    def down_step():
        down_copy.wait_recv()

        @pl.when(not_first)
        def _():
            down_send[...] = down_recv[...] + res[...]
            down_copy.start()

    @pl.when(k_idx == 0)
    def _():
        up_recv[...] = jnp.zeros_like(up_recv)
        up_send[...] = res[...]
        up_copy.start()

    @pl.when(k_idx == n - 1)
    def _():
        down_recv[...] = jnp.zeros_like(down_recv)
        down_send[...] = res[...]
        down_copy.start()

    own_rows = jnp.concatenate([rows_for(pw, c) for pw in order], axis=0)
    copy_wo.wait()
    part_keep[...] = dot(own_rows, wo_own[...])
    wo_copy.wait_recv()
    nh_copy.wait_recv()

    def win_copies(send, recv, send_sem, recv_sem):
        return [
            remote(send.at[i], recv.at[i], send_sem.at[i], recv_sem.at[i], {"win": pw})
            for i, pw in enumerate((side, across) * 2 + (across, side))
        ]

    part_copies = win_copies(part_send, part_recv, part_send_sem, part_recv_sem)
    model = hidden.shape[1]
    part_cols = model // 2

    def relay(copies, send, recv, cols, far_term, side_term, across_term, own_term):
        term = far_term().astype(BF16)
        send[0] = term[:, :cols]
        copies[0].start()
        send[1] = term[:, cols:]
        copies[1].start()
        term = side_term()
        send[2] = term[:, :cols].astype(BF16)
        copies[2].start()
        side_rest = term[:, cols:]
        term = across_term()
        send[3] = term[:, cols:].astype(BF16)
        copies[3].start()
        across_rest = term[:, :cols]
        own = own_term()
        copies[0].wait_recv()
        send[4] = (across_rest + recv[0].astype(F32)).astype(BF16)
        copies[4].start()
        copies[1].wait_recv()
        send[5] = (side_rest + recv[1].astype(F32)).astype(BF16)
        copies[5].start()
        return own

    part_all = part_keep[...] + dot(nh_recv[...], wo_sib[...])
    part_terms = [part_all[i * blk : (i + 1) * blk] for i in range(wins)]
    own_part = relay(
        part_copies, part_send, part_recv, part_cols,
        lambda: part_terms[3], lambda: part_terms[1], lambda: part_terms[2],
        lambda: part_terms[0] + hidden[...].astype(F32),
    )

    for cp in part_copies[2:]:
        cp.wait_recv()
    summed = own_part + jnp.concatenate(
        [part_recv[2 + i].astype(F32) + part_recv[4 + i].astype(F32) for i in range(2)], axis=1
    )
    stream_out[...] = summed.astype(BF16)
    stream_copy = pltpu.make_async_copy(stream_out, stream_hbm, local_sem.at[2])
    stream_copy.start()
    scale = lax.rsqrt(jnp.mean(summed * summed, axis=-1, keepdims=True) + 1e-5)
    ns[...] = (summed * scale * norm_gain[...]).astype(BF16)
    in_block = wq.shape[0]
    my_rows = pl.ds(pl.multiple_of(me * blk, blk), blk)
    ns_copies = []
    for pw in (far, side, across):
        for pc in (c, 1 - c):
            i = len(ns_copies)
            cp = remote(
                ns.at[:, pl.ds(pl.multiple_of(pw * in_block, in_block), in_block)],
                gathered.at[my_rows, :],
                ns_send_sem.at[i], ns_recv_sem.at[i], {"win": pw, "wout": pc},
            )
            cp.start()
            ns_copies.append(cp)
    last = len(ns_copies)
    cp = remote(
        ns.at[:, pl.ds(pl.multiple_of(w * in_block, in_block), in_block)],
        gathered.at[my_rows, :],
        ns_send_sem.at[last], ns_recv_sem.at[last], sib,
    )
    cp.start()
    ns_copies.append(cp)
    gathered[my_rows, :] = ns[:, pl.ds(pl.multiple_of(w * in_block, in_block), in_block)]

    pl.when(k_idx == 1)(up_step)
    pl.when(k_idx == n - 2)(down_step)

    copy_wq.wait()
    out_rows = blk * 2
    cols = wq.shape[1] // 2

    def project(pw, arriving):
        for cp in arriving:
            cp.wait_recv()
        block = gathered[pl.ds(pl.multiple_of(pw * out_rows, out_rows), out_rows), :]
        return dot(block, wq[...])

    proj_copies = win_copies(proj_send, proj_recv, proj_send_sem, proj_recv_sem)
    own = relay(
        proj_copies, proj_send, proj_recv, cols,
        lambda: project(far, ns_copies[0:2]), lambda: project(side, ns_copies[2:4]),
        lambda: project(across, ns_copies[4:6]), lambda: project(w, ns_copies[6:]),
    )

    pl.when((k_idx == 2) & (k_idx > 1))(up_step)
    pl.when((k_idx == n - 3) & (k_idx < n - 2))(down_step)
    pl.when(k_idx > 2)(up_step)
    pl.when(k_idx < n - 3)(down_step)

    total_res = res[...].astype(F32) + up_recv[...].astype(F32) + down_recv[...].astype(F32)
    fs_out[...] = total_res[:edge_base].astype(BF16)
    fs_copy = pltpu.make_async_copy(fs_out, fs_hbm, local_sem.at[3])
    fs_copy.start()
    for t in range(3 * pieces):
        base = edge_base + t * 16
        edge_out[:, t * DK : (t + 1) * DK] = total_res[base : base + 16]

    for cp in proj_copies[2:]:
        cp.wait_recv()
    for i, part in enumerate((slice(0, cols), slice(cols, 2 * cols))):
        qkv_next[:, part] = (
            own[:, part] + proj_recv[2 + i].astype(F32) + proj_recv[4 + i].astype(F32)
        ).astype(BF16)

    stream_copy.wait()
    fs_copy.wait()
    wo_copy.wait_send()
    nh_copy.wait_send()
    for cp in part_copies + ns_copies + proj_copies:
        cp.wait_send()

    @pl.when(not_last)
    def _():
        halo_copy.wait_send()
        for cp in [x for pair in state_copies for x in pair]:
            cp.wait_send()
        up_copy.wait_send()

    @pl.when(not_first)
    def _():
        down_copy.wait_send()


def place_results(
    reqs, taps, width,
    qkv_next, stream_out, states, edges,
    qkv_next_out, stream_out_out, states_out, edges_out,
    qkv_held, stream_held, states_held, states_wide, edges_held, sems,
):
    held = (qkv_held, stream_held, states_held)
    arrive = [
        pltpu.make_async_copy(src, dst, sems.at[i])
        for i, (src, dst) in enumerate(zip((qkv_next, stream_out, states), held))
    ]
    leave = [
        pltpu.make_async_copy(src, dst, sems.at[3 + i])
        for i, (src, dst) in enumerate(
            zip((qkv_held, stream_held, states_wide, edges_held), (qkv_next_out, stream_out_out, states_out, edges_out))
        )
    ]
    for i in (2, 0, 1):
        arrive[i].start()
    for i in range(taps):
        for t in range(3):
            edges_held[i, t] = edges[
                i * reqs : (i + 1) * reqs, t * width : (t + 1) * width
            ].astype(BF16)
    leave[3].start()
    arrive[2].wait()
    states_wide[...] = states_held[...].astype(F32)
    leave[2].start()
    for i in range(2):
        arrive[i].wait()
        leave[i].start()
    for cp in leave:
        cp.wait()


def solution(mesh):
    n, wins = mesh.shape["seq"], mesh.shape["win"]

    def body(qkv_in, conv_w, beta_logits, lengths, out_gain, w_out, hidden_in, norm_gain, w_qkv):
        rows, _, width = qkv_in.shape
        heads = width // DK
        reqs = lengths.shape[0]
        blk, model = hidden_in.shape
        in_block, out_cols = w_qkv.shape
        group = wins * 2
        res_rows = reqs * heads * DK + 16 * 3 * (width // DK)
        vmem = pl.BlockSpec(memory_space=pltpu.VMEM)
        place = pl.BlockSpec(memory_space=pl.ANY)
        dma = pltpu.SemaphoreType.DMA
        results = pl.pallas_call(
            functools.partial(kernel, n, wins, reqs),
            out_shape=(
                jax.ShapeDtypeStruct((blk * 2, out_cols), BF16),
                jax.ShapeDtypeStruct((blk, model), BF16),
                jax.ShapeDtypeStruct((reqs * heads * DK, DK), BF16),
                jax.ShapeDtypeStruct((16, 3 * width), F32),
            ),
            in_specs=[pl.BlockSpec(memory_space=pltpu.SMEM)] + [vmem] * 6
            + [pl.BlockSpec(memory_space=pl.ANY)] * 2,
            out_specs=(vmem, place, place, vmem),
            scratch_shapes=[
                pltpu.VMEM((blk, model), BF16),
                pltpu.VMEM((reqs * heads * DK, DK), BF16),
                pltpu.VMEM((3, HALO, width), BF16),
                pltpu.VMEM((width, model), BF16),
                pltpu.VMEM((width, model), BF16),
                pltpu.VMEM((in_block, out_cols), BF16),
                pltpu.VMEM((n // 2, heads * DK, DK), BF16),
                pltpu.VMEM((n // 2, heads * DK, DK), BF16),
                pltpu.VMEM((rows, width), BF16),
                pltpu.VMEM((rows // 2, width), BF16),
                pltpu.VMEM((rows // 2, width), BF16),
                pltpu.VMEM((rows // 2, model), F32),
                pltpu.VMEM((6, blk, model // 2), BF16),
                pltpu.VMEM((6, blk, model // 2), BF16),
                pltpu.VMEM((blk, model), BF16),
                pltpu.VMEM((rows, in_block), BF16),
                pltpu.VMEM((6, blk * 2, out_cols // 2), BF16),
                pltpu.VMEM((6, blk * 2, out_cols // 2), BF16),
                pltpu.VMEM((res_rows, DK), BF16),
                pltpu.VMEM((res_rows, DK), BF16),
                pltpu.VMEM((res_rows, DK), BF16),
                pltpu.VMEM((res_rows, DK), BF16),
                pltpu.VMEM((res_rows, DK), BF16),
                dma((4,)), dma((2,)), dma((2,)), dma((2, n // 2 * heads)), dma((2,)),
                dma((6,)), dma((6,)), dma((group,)), dma((group,)),
                dma((6,)), dma((6,)), dma((2,)), dma((2,)),
            ],
            compiler_params=pltpu.CompilerParams(
                collective_id=0, has_side_effects=True, vmem_limit_bytes=56 * 1024 * 1024
            ),
            cost_estimate=pl.CostEstimate(
                flops=4 * 10**9, bytes_accessed=8 * 10**6, transcendentals=10**6
            ),
            name="delta_sublayer",
        )(
            lengths, jnp.transpose(qkv_in, (1, 0, 2)), conv_w, beta_logits,
            out_gain.reshape(1, DK), hidden_in, norm_gain.reshape(1, model), w_out, w_qkv,
        )
        taps = CONV - 1
        projected, stream, states, edges = pl.pallas_call(
            functools.partial(place_results, reqs, taps, width),
            out_shape=tuple(jax.ShapeDtypeStruct(x.shape, x.dtype) for x in results[:2])
            + (jax.ShapeDtypeStruct(results[2].shape, F32),)
            + (jax.ShapeDtypeStruct((taps, 3, reqs, width), BF16),),
            in_specs=[place] * 3 + [vmem],
            out_specs=(place,) * 4,
            scratch_shapes=[pltpu.VMEM(x.shape, x.dtype) for x in results[:3]]
            + [pltpu.VMEM(results[2].shape, F32)]
            + [pltpu.VMEM((taps, 3, reqs, width), BF16), dma((7,))],
            compiler_params=pltpu.CompilerParams(vmem_limit_bytes=60 * 1024 * 1024),
            name="place_results",
        )(*results)
        return projected, stream, states.reshape(reqs, heads, DK, DK), jnp.transpose(edges, (2, 0, 1, 3))

    return jax.shard_map(
        body,
        mesh=mesh,
        in_specs=(
            P("seq", None, ("win", "wout")),
            P(None, None, ("win", "wout")),
            P(("win", "wout"), "seq"),
            P(),
            P(),
            P(("win", "wout"), None),
            P(("seq", "win", "wout"), None),
            P(),
            P("win", "wout"),
        ),
        out_specs=(
            P(("seq", "win"), "wout"),
            P(("seq", "win", "wout"), None),
            P(None, ("win", "wout"), None, None),
            P(None, None, None, ("win", "wout")),
        ),
        check_vma=False,
    )
```

```python
import functools

import jax
import jax.numpy as jnp
from jax import lax
from jax.experimental import pallas as pl
from jax.experimental.pallas import tpu as pltpu
from jax.sharding import PartitionSpec as P

MESH = pl.DeviceIdType.MESH
DK = 128
CONV = 4
HALO = 16
F32 = jnp.float32
BF16 = jnp.bfloat16


def dot(a, b):
    return jnp.dot(a, b, preferred_element_type=F32)


def dot_t(a, b):
    return lax.dot_general(a, b, (((1,), (1,)), ((), ())), preferred_element_type=F32)


def split(x):
    high = x.astype(BF16)
    return high, (x - high.astype(F32)).astype(BF16)


def mm3(a, b):
    ah, al = split(a)
    bh, bl = split(b)
    return dot(ah, bh) + (dot(ah, bl) + dot(al, bh))


def mm1(a, b):
    return dot(a.astype(BF16), b.astype(BF16))


def mm_left(a, b):
    high, low = split(a)
    return dot(high, b) + dot(low, b)


def mm_right(a, b):
    high, low = split(b)
    return dot(a, high) + dot(a, low)


def kernel(
    n, wins, reqs,
    lengths, qkv_hbm, conv_w_hbm, beta_hbm, out_gain_hbm, hidden_hbm, norm_gain_hbm, w_out, w_qkv,
    qkv_next, stream_hbm, fs_hbm, edge_out,
    qkv, conv_w, beta, out_gain, hidden, norm_gain, stream_out, fs_out, halo, wo_own, wo_sib, wq, state_send, state_recv, nh, nh_send, nh_recv,
    part_keep, part_send, part_recv, ns, gathered, proj_send, proj_recv,
    res, up_send, up_recv, down_send, down_recv,
    local_sem, load_sem, halo_sem, wo_sem, state_sem, nh_sem, part_send_sem, part_recv_sem,
    ns_send_sem, ns_recv_sem, proj_send_sem, proj_recv_sem, up_sem, down_sem,
):
    rows = qkv.shape[1]
    width = qkv.shape[2]
    heads = width // DK
    half = rows // 2
    group = wins * 2
    blk = hidden.shape[0]
    k_idx = lax.axis_index("seq")
    w = lax.axis_index("win")
    c = lax.axis_index("wout")
    me = w * 2 + c
    sib = {"wout": 1 - c}
    above = {"seq": lax.rem(k_idx + 1, n)}
    below = {"seq": lax.rem(k_idx + n - 1, n)}
    not_first = k_idx > 0
    not_last = k_idx < n - 1

    def remote(src, dst, send_sem, recv_sem, device):
        return pltpu.make_async_remote_copy(
            src_ref=src, dst_ref=dst, send_sem=send_sem, recv_sem=recv_sem,
            device_id=device, device_id_type=MESH,
        )

    def peer(o):
        p = lax.rem(me + o, group)
        return p // 2, lax.rem(p, 2)

    barrier = pltpu.get_barrier_semaphore()
    for o in range(1, group):
        pw, pc = peer(o)
        pl.semaphore_signal(barrier, inc=1, device_id={"win": pw, "wout": pc}, device_id_type=MESH)

    @pl.when(not_first)
    def _():
        pl.semaphore_signal(barrier, inc=1, device_id=below, device_id_type=MESH)

    @pl.when(not_last)
    def _():
        pl.semaphore_signal(barrier, inc=1, device_id=above, device_id_type=MESH)

    loads = [
        pltpu.make_async_copy(src, dst, load_sem.at[i])
        for i, (src, dst) in enumerate((
            (qkv_hbm, qkv), (conv_w_hbm, conv_w), (beta_hbm, beta),
            (out_gain_hbm, out_gain), (hidden_hbm, hidden), (norm_gain_hbm, norm_gain),
        ))
    ]
    for cp in loads:
        cp.start()
    copy_wo = pltpu.make_async_copy(w_out, wo_own, local_sem.at[0])
    copy_wq = pltpu.make_async_copy(w_qkv, wq, local_sem.at[1])
    copy_wo.start()
    copy_wq.start()
    ends = []
    total = jnp.int32(0)
    for r in range(reqs):
        total = total + lengths[r]
        ends.append(total)
    first = k_idx * rows

    def segments(positions):
        seg = jnp.zeros_like(positions)
        for r in range(reqs):
            seg = seg + (positions >= ends[r]).astype(jnp.int32)
        return jnp.where(positions < 0, -1, seg)

    def scalar_segment(position):
        seg = jnp.int32(0)
        for r in range(reqs):
            seg = seg + (position >= ends[r]).astype(jnp.int32)
        return jnp.where(position < 0, -1, seg)

    col_pos = first + lax.broadcasted_iota(jnp.int32, (rows, 1), 0)
    row_pos = first + lax.broadcasted_iota(jnp.int32, (1, rows), 1)
    col_seg = segments(col_pos)
    row_seg = segments(row_pos)
    before_seg = scalar_segment(first - 1)
    last_seg = scalar_segment(first + rows - 1)
    coupled = (col_seg == before_seg).astype(F32)
    in_last = (row_seg == last_seg).astype(F32)
    last_link = (before_seg == last_seg).astype(F32)

    ri = lax.broadcasted_iota(jnp.int32, (rows, rows), 0)
    ci = lax.broadcasted_iota(jnp.int32, (rows, rows), 1)
    same = col_seg == row_seg
    causal = same & (ri >= ci)
    strict = same & (ri > ci)
    diagonal = ri == ci
    hi_ = lax.broadcasted_iota(jnp.int32, (half, half), 0)
    hj_ = lax.broadcasted_iota(jnp.int32, (half, half), 1)
    eye_half = (hi_ == hj_).astype(F32)
    eye_keys = (
        lax.broadcasted_iota(jnp.int32, (DK, DK), 0) == lax.broadcasted_iota(jnp.int32, (DK, DK), 1)
    ).astype(F32)

    def silu(x):
        return (x / (1.0 + jnp.exp(-x))).astype(BF16).astype(F32)

    index_col = lax.broadcasted_iota(jnp.int32, (rows, 1), 0)
    keeps = [None] + [segments(col_pos - back) == col_seg for back in range(1, CONV)]

    def tap(t, back):
        return conv_w[t, CONV - 1 - back : CONV - back, :]

    pres = []
    mains = []
    def convolve(t):
        wide = qkv[t].astype(F32)
        pre = tap(t, 0) * wide
        for back in range(1, CONV):
            shifted = pltpu.roll(wide, back, axis=0)
            pre = pre + tap(t, back) * jnp.where(keeps[back] & (index_col >= back), shifted, 0.0)
        pres.append(pre[:8])
        mains.append(silu(pre)[8:])

    loads[0].wait()
    loads[1].wait()
    convolve(0)
    pl.semaphore_wait(
        barrier, group - 1 + not_first.astype(jnp.int32) + not_last.astype(jnp.int32)
    )

    halo_copy = remote(
        qkv_hbm.at[:, pl.ds(rows - HALO, HALO), :], halo, halo_sem.at[0], halo_sem.at[1], above
    )

    @pl.when(not_last)
    def _():
        halo_copy.start()

    wo_copy = remote(w_out, wo_sib, wo_sem.at[0], wo_sem.at[1], sib)
    wo_copy.start()

    @pl.when(jnp.logical_not(not_first))
    def _():
        halo[...] = jnp.zeros_like(halo)
        state_recv[...] = jnp.zeros_like(state_recv)

    convolve(1)
    convolve(2)
    loads[2].wait()
    strength = []
    for h in range(heads):
        b_row = 1.0 / (1.0 + jnp.exp(-beta[h : h + 1, :]))
        strength.append(jnp.sum(jnp.where(diagonal, b_row, 0.0), axis=1, keepdims=True))

    @pl.when(not_first)
    def _():
        halo_copy.wait_recv()

    activated = []
    for t in range(3):
        rim = halo[t].astype(F32)[HALO - 8 :]
        pre = pres[t]
        for back in range(1, CONV):
            shifted = pltpu.roll(rim, back, axis=0)
            pre = pre + tap(t, back) * jnp.where(
                keeps[back][:8] & (index_col[:8] < back), shifted, 0.0
            )
        activated.append(jnp.concatenate([silu(pre), mains[t]], axis=0))

    def norm_factor(x, axis):
        return lax.rsqrt(jnp.sum(x * x, axis=axis, keepdims=True) + 1e-6)

    q, k, v, kt, k_col, a_full, scores = [], [], [], [], [], [], []
    for h in range(heads):
        cols = slice(h * DK, (h + 1) * DK)
        q_raw, k_raw = activated[0][:, cols], activated[1][:, cols]
        q_col = norm_factor(q_raw, 1)
        k_col.append(norm_factor(k_raw, 1))
        kt_raw = jnp.transpose(k_raw)
        k_row = norm_factor(kt_raw, 0)
        q.append(q_raw * q_col)
        k.append(k_raw * k_col[h])
        v.append(activated[2][:, cols])
        kt.append(kt_raw)
        k_half = k_raw.astype(BF16)
        gram = dot_t(k_half, k_half) * k_row
        a_full.append(jnp.where(strict, (strength[h] * k_col[h]) * gram, 0.0))
        scores.append(
            jnp.where(causal, q_col * (dot_t(q_raw.astype(BF16), k_half) * k_row), 0.0)
        )

    diag = []
    for h in range(heads):
        diag.append(a_full[h][:half, :half])
        diag.append(a_full[h][half:, half:])
    level = 0
    inverse = None
    while (1 << level) < half:
        pick = (
            ((hi_ >> (level + 1)) == (hj_ >> (level + 1)))
            & (((hi_ >> level) & 1) == 1)
            & (((hj_ >> level) & 1) == 0)
        )
        lower = [jnp.where(pick, a, 0.0) for a in diag]
        if level == 0:
            inverse = [eye_half - x for x in lower]
        else:
            ys = [mm1(x, z) for x, z in zip(lower, inverse)]
            inverse = [z - mm1(z, y) for z, y in zip(inverse, ys)]
        level += 1

    solved, out_local, q_link, trans, write = [], [], [], [], []
    for h in range(heads):
        rhs = jnp.concatenate([strength[h] * v[h], (strength[h] * coupled) * k[h]], axis=1)
        top = mm3(inverse[2 * h], rhs[:half])
        low = mm3(inverse[2 * h + 1], rhs[half:] - mm1(a_full[h][half:, :half], top))
        solved.append(jnp.concatenate([top, low], axis=0))
    for h in range(heads):
        m = mm_right((kt[h] * in_last).astype(BF16), k_col[h] * solved[h])
        write.append(m[:, :DK])
        trans.append(last_link * (eye_keys - m[:, DK:]))

    steps = n // 2
    state_copies = [
        [
            remote(
                state_send.at[i, pl.ds(h * DK, DK)], state_recv.at[i, pl.ds(h * DK, DK)],
                state_sem.at[0, i * heads + h], state_sem.at[1, i * heads + h], above,
            )
            for h in range(heads)
        ]
        for i in range(steps)
    ]
    for i in range(steps):
        for h in range(heads):
            hr = slice(h * DK, (h + 1) * DK)
            state = write[h]
            if i > 0:
                pl.when(not_first)(state_copies[i - 1][h].wait_recv)
                state = state + mm_left(trans[h], state_recv[i - 1, hr, :])
            state_send[i, hr, :] = state.astype(BF16)
            pl.when(not_last)(state_copies[i][h].start)
        if i == 0:
            local = [mm1(scores[h], solved[h]) for h in range(heads)]
            links = [coupled * q[h] - local[h][:, DK:] for h in range(heads)]
    state_in = []

    loads[3].wait()
    corrected = []
    for h in range(heads):
        pl.when(not_first)(state_copies[steps - 1][h].wait_recv)
        state_in.append(state_recv[steps - 1, h * DK : (h + 1) * DK, :])
        att = local[h][:, :DK] + dot(links[h].astype(BF16), state_in[h])
        corrected.append(k_col[h] * (solved[h][:, :DK] - mm_left(solved[h][:, DK:], state_in[h])))
        scale = lax.rsqrt(jnp.mean(att * att, axis=-1, keepdims=True) + 1e-5)
        nh[:, h * DK : (h + 1) * DK] = (att * scale * out_gain[...]).astype(BF16)

    wy, wx = w // 2, lax.rem(w, 2)
    side, across, far = wy * 2 + (1 - wx), (1 - wy) * 2 + wx, 3 - w
    order = (w, side, across, far)

    def rows_for(pw, pc):
        return nh[pl.ds(pl.multiple_of((2 * pw + pc) * blk, blk), blk), :]

    for i, pw in enumerate(order):
        nh_send[i * blk : (i + 1) * blk, :] = rows_for(pw, 1 - c)
    nh_copy = remote(nh_send, nh_recv, nh_sem.at[0], nh_sem.at[1], sib)
    nh_copy.start()

    for r in range(reqs):
        owned = (ends[r] - 1 >= first) & (ends[r] - 1 < first + rows)
        owned_f = owned.astype(F32)
        member = (row_seg == r).astype(F32) * owned_f
        carry = owned_f * (before_seg == r).astype(F32)
        for h in range(heads):
            base = (r * heads + h) * DK
            res[base : base + DK, :] = (
                mm_right((kt[h] * member).astype(BF16), corrected[h])
                + carry * state_in[h].astype(F32)
            ).astype(BF16)
    edge_base = reqs * heads * DK

    def selection(base, count):
        sel_row = lax.broadcasted_iota(jnp.int32, (16, count), 0)
        sel_pos = base + lax.broadcasted_iota(jnp.int32, (16, count), 1)
        sel_seg = segments(sel_pos)
        select = jnp.zeros((16, count), F32)
        for r in range(reqs):
            owned = (ends[r] - 1 >= first) & (ends[r] - 1 < first + rows)
            for i in range(CONV - 1):
                hit = (
                    (sel_row == i * reqs + r)
                    & (sel_pos == ends[r] - (CONV - 1) + i)
                    & (sel_seg == r)
                )
                select = select + jnp.where(hit, 1.0, 0.0) * owned.astype(F32)
        return select.astype(BF16)

    select_halo = selection(first - HALO, HALO)
    select_own = selection(first, rows)
    pieces = width // DK
    for t in range(3):
        edge = dot(select_halo, halo[t]) + dot(select_own, qkv[t])
        for j in range(pieces):
            base = edge_base + (t * pieces + j) * 16
            res[base : base + 16, :] = edge[:, j * DK : (j + 1) * DK].astype(BF16)

    up_copy = remote(up_send, up_recv, up_sem.at[0], up_sem.at[1], above)
    down_copy = remote(down_send, down_recv, down_sem.at[0], down_sem.at[1], below)

    def up_step():
        up_copy.wait_recv()

        @pl.when(not_last)
        def _():
            up_send[...] = up_recv[...] + res[...]
            up_copy.start()

    def down_step():
        down_copy.wait_recv()

        @pl.when(not_first)
        def _():
            down_send[...] = down_recv[...] + res[...]
            down_copy.start()

    @pl.when(k_idx == 0)
    def _():
        up_recv[...] = jnp.zeros_like(up_recv)
        up_send[...] = res[...]
        up_copy.start()

    @pl.when(k_idx == n - 1)
    def _():
        down_recv[...] = jnp.zeros_like(down_recv)
        down_send[...] = res[...]
        down_copy.start()

    own_rows = jnp.concatenate([rows_for(pw, c) for pw in order], axis=0)
    copy_wo.wait()
    part_keep[...] = dot(own_rows, wo_own[...])
    wo_copy.wait_recv()
    nh_copy.wait_recv()

    def win_copies(send, recv, send_sem, recv_sem):
        return [
            remote(send.at[i], recv.at[i], send_sem.at[i], recv_sem.at[i], {"win": pw})
            for i, pw in enumerate((side, across) * 2 + (across, side))
        ]

    part_copies = win_copies(part_send, part_recv, part_send_sem, part_recv_sem)
    model = hidden.shape[1]
    part_cols = model // 2

    def relay(copies, send, recv, far_term, side_term, across_term, own_term):
        for i in range(2):
            send[i] = far_term(i).astype(BF16)
            copies[i].start()
        send[2] = side_term(0).astype(BF16)
        copies[2].start()
        send[3] = across_term(1).astype(BF16)
        copies[3].start()
        across_rest = across_term(0)
        side_rest = side_term(1)
        copies[0].wait_recv()
        send[4] = (across_rest + recv[0].astype(F32)).astype(BF16)
        copies[4].start()
        copies[1].wait_recv()
        send[5] = (side_rest + recv[1].astype(F32)).astype(BF16)
        copies[5].start()
        return own_term()

    loads[4].wait()
    loads[5].wait()
    part_all = part_keep[...] + dot(nh_recv[...], wo_sib[...])

    def part_term(i):
        return lambda j: part_all[i * blk : (i + 1) * blk, j * part_cols : (j + 1) * part_cols]

    own_part = relay(
        part_copies, part_send, part_recv, part_term(3), part_term(1), part_term(2),
        lambda: part_all[:blk] + hidden[...].astype(F32),
    )

    for cp in part_copies[2:]:
        cp.wait_recv()
    summed = own_part + jnp.concatenate(
        [part_recv[2 + i].astype(F32) + part_recv[4 + i].astype(F32) for i in range(2)], axis=1
    )
    stream_out[...] = summed.astype(BF16)
    stream_copy = pltpu.make_async_copy(stream_out, stream_hbm, local_sem.at[2])
    stream_copy.start()
    scale = lax.rsqrt(jnp.mean(summed * summed, axis=-1, keepdims=True) + 1e-5)
    ns[...] = (summed * scale * norm_gain[...]).astype(BF16)
    in_block = wq.shape[0]
    my_rows = pl.ds(pl.multiple_of(me * blk, blk), blk)
    ns_copies = []
    for pw in (far, side, across):
        for pc in (c, 1 - c):
            i = len(ns_copies)
            cp = remote(
                ns.at[:, pl.ds(pl.multiple_of(pw * in_block, in_block), in_block)],
                gathered.at[my_rows, :],
                ns_send_sem.at[i], ns_recv_sem.at[i], {"win": pw, "wout": pc},
            )
            cp.start()
            ns_copies.append(cp)
    last = len(ns_copies)
    cp = remote(
        ns.at[:, pl.ds(pl.multiple_of(w * in_block, in_block), in_block)],
        gathered.at[my_rows, :],
        ns_send_sem.at[last], ns_recv_sem.at[last], sib,
    )
    cp.start()
    ns_copies.append(cp)
    gathered[my_rows, :] = ns[:, pl.ds(pl.multiple_of(w * in_block, in_block), in_block)]

    pl.when(k_idx == 1)(up_step)
    pl.when(k_idx == n - 2)(down_step)

    copy_wq.wait()
    out_rows = blk * 2
    cols = wq.shape[1] // 2

    def project(pw, arriving):
        block_rows = pl.ds(pl.multiple_of(pw * out_rows, out_rows), out_rows)
        pending = list(arriving)

        def term(j):
            while pending:
                pending.pop().wait_recv()
            return dot(gathered[block_rows, :], wq[:, j * cols : (j + 1) * cols])

        return term

    proj_copies = win_copies(proj_send, proj_recv, proj_send_sem, proj_recv_sem)
    own_term = project(w, ns_copies[6:])
    own = relay(
        proj_copies, proj_send, proj_recv, project(far, ns_copies[0:2]),
        project(side, ns_copies[2:4]), project(across, ns_copies[4:6]),
        lambda: (own_term(0), own_term(1)),
    )

    pl.when((k_idx == 2) & (k_idx > 1))(up_step)
    pl.when((k_idx == n - 3) & (k_idx < n - 2))(down_step)
    pl.when(k_idx > 2)(up_step)
    pl.when(k_idx < n - 3)(down_step)

    total_res = res[...].astype(F32) + up_recv[...].astype(F32) + down_recv[...].astype(F32)
    fs_out[...] = total_res[:edge_base].astype(BF16)
    fs_copy = pltpu.make_async_copy(fs_out, fs_hbm, local_sem.at[3])
    fs_copy.start()
    for t in range(3 * pieces):
        base = edge_base + t * 16
        edge_out[:, t * DK : (t + 1) * DK] = total_res[base : base + 16]

    for cp in proj_copies[2:]:
        cp.wait_recv()
    for i, part in enumerate((slice(0, cols), slice(cols, 2 * cols))):
        qkv_next[:, part] = (
            own[i] + proj_recv[2 + i].astype(F32) + proj_recv[4 + i].astype(F32)
        ).astype(BF16)

    stream_copy.wait()
    fs_copy.wait()
    wo_copy.wait_send()
    nh_copy.wait_send()
    for cp in part_copies + ns_copies + proj_copies:
        cp.wait_send()

    @pl.when(not_last)
    def _():
        halo_copy.wait_send()
        for cp in [x for pair in state_copies for x in pair]:
            cp.wait_send()
        up_copy.wait_send()

    @pl.when(not_first)
    def _():
        down_copy.wait_send()


def place_results(
    reqs, taps, width,
    qkv_next, stream_out, states, edges,
    qkv_next_out, stream_out_out, states_out, edges_out,
    qkv_held, stream_held, states_held, states_wide, edges_held, sems,
):
    held = (qkv_held, stream_held, states_held)
    arrive = [
        pltpu.make_async_copy(src, dst, sems.at[i])
        for i, (src, dst) in enumerate(zip((qkv_next, stream_out, states), held))
    ]
    leave = [
        pltpu.make_async_copy(src, dst, sems.at[3 + i])
        for i, (src, dst) in enumerate(
            zip((qkv_held, stream_held, states_wide, edges_held), (qkv_next_out, stream_out_out, states_out, edges_out))
        )
    ]
    for i in (2, 0, 1):
        arrive[i].start()
    for i in range(taps):
        for t in range(3):
            edges_held[i, t] = edges[
                i * reqs : (i + 1) * reqs, t * width : (t + 1) * width
            ].astype(BF16)
    leave[3].start()
    arrive[2].wait()
    states_wide[...] = states_held[...].astype(F32)
    leave[2].start()
    for i in range(2):
        arrive[i].wait()
        leave[i].start()
    for cp in leave:
        cp.wait()


def solution(mesh):
    n, wins = mesh.shape["seq"], mesh.shape["win"]

    def body(qkv_in, conv_w, beta_logits, lengths, out_gain, w_out, hidden_in, norm_gain, w_qkv):
        rows, _, width = qkv_in.shape
        heads = width // DK
        reqs = lengths.shape[0]
        blk, model = hidden_in.shape
        in_block, out_cols = w_qkv.shape
        group = wins * 2
        res_rows = reqs * heads * DK + 16 * 3 * (width // DK)
        vmem = pl.BlockSpec(memory_space=pltpu.VMEM)
        place = pl.BlockSpec(memory_space=pl.ANY)
        dma = pltpu.SemaphoreType.DMA
        results = pl.pallas_call(
            functools.partial(kernel, n, wins, reqs),
            out_shape=(
                jax.ShapeDtypeStruct((blk * 2, out_cols), BF16),
                jax.ShapeDtypeStruct((blk, model), BF16),
                jax.ShapeDtypeStruct((reqs * heads * DK, DK), BF16),
                jax.ShapeDtypeStruct((16, 3 * width), F32),
            ),
            in_specs=[pl.BlockSpec(memory_space=pltpu.SMEM)] + [place] * 8,
            out_specs=(vmem, place, place, vmem),
            scratch_shapes=[
                pltpu.VMEM((3, rows, width), BF16),
                pltpu.VMEM(conv_w.shape, F32),
                pltpu.VMEM(beta_logits.shape, F32),
                pltpu.VMEM((1, DK), F32),
                pltpu.VMEM((blk, model), BF16),
                pltpu.VMEM((1, model), F32),
                pltpu.VMEM((blk, model), BF16),
                pltpu.VMEM((reqs * heads * DK, DK), BF16),
                pltpu.VMEM((3, HALO, width), BF16),
                pltpu.VMEM((width, model), BF16),
                pltpu.VMEM((width, model), BF16),
                pltpu.VMEM((in_block, out_cols), BF16),
                pltpu.VMEM((n // 2, heads * DK, DK), BF16),
                pltpu.VMEM((n // 2, heads * DK, DK), BF16),
                pltpu.VMEM((rows, width), BF16),
                pltpu.VMEM((rows // 2, width), BF16),
                pltpu.VMEM((rows // 2, width), BF16),
                pltpu.VMEM((rows // 2, model), F32),
                pltpu.VMEM((6, blk, model // 2), BF16),
                pltpu.VMEM((6, blk, model // 2), BF16),
                pltpu.VMEM((blk, model), BF16),
                pltpu.VMEM((rows, in_block), BF16),
                pltpu.VMEM((6, blk * 2, out_cols // 2), BF16),
                pltpu.VMEM((6, blk * 2, out_cols // 2), BF16),
                pltpu.VMEM((res_rows, DK), BF16),
                pltpu.VMEM((res_rows, DK), BF16),
                pltpu.VMEM((res_rows, DK), BF16),
                pltpu.VMEM((res_rows, DK), BF16),
                pltpu.VMEM((res_rows, DK), BF16),
                dma((4,)), dma((6,)), dma((2,)), dma((2,)), dma((2, n // 2 * heads)), dma((2,)),
                dma((6,)), dma((6,)), dma((group,)), dma((group,)),
                dma((6,)), dma((6,)), dma((2,)), dma((2,)),
            ],
            compiler_params=pltpu.CompilerParams(
                collective_id=0, has_side_effects=True, vmem_limit_bytes=56 * 1024 * 1024
            ),
            cost_estimate=pl.CostEstimate(
                flops=4 * 10**9, bytes_accessed=8 * 10**6, transcendentals=10**6
            ),
            name="delta_sublayer",
        )(
            lengths, jnp.transpose(qkv_in, (1, 0, 2)), conv_w, beta_logits,
            out_gain.reshape(1, DK), hidden_in, norm_gain.reshape(1, model), w_out, w_qkv,
        )
        taps = CONV - 1
        projected, stream, states, edges = pl.pallas_call(
            functools.partial(place_results, reqs, taps, width),
            out_shape=tuple(jax.ShapeDtypeStruct(x.shape, x.dtype) for x in results[:2])
            + (jax.ShapeDtypeStruct(results[2].shape, F32),)
            + (jax.ShapeDtypeStruct((taps, 3, reqs, width), BF16),),
            in_specs=[place] * 3 + [vmem],
            out_specs=(place,) * 4,
            scratch_shapes=[pltpu.VMEM(x.shape, x.dtype) for x in results[:3]]
            + [pltpu.VMEM(results[2].shape, F32)]
            + [pltpu.VMEM((taps, 3, reqs, width), BF16), dma((7,))],
            compiler_params=pltpu.CompilerParams(vmem_limit_bytes=60 * 1024 * 1024),
            name="place_results",
        )(*results)
        return projected, stream, states.reshape(reqs, heads, DK, DK), jnp.transpose(edges, (2, 0, 1, 3))

    return jax.shard_map(
        body,
        mesh=mesh,
        in_specs=(
            P("seq", None, ("win", "wout")),
            P(None, None, ("win", "wout")),
            P(("win", "wout"), "seq"),
            P(),
            P(),
            P(("win", "wout"), None),
            P(("seq", "win", "wout"), None),
            P(),
            P("win", "wout"),
        ),
        out_specs=(
            P(("seq", "win"), "wout"),
            P(("seq", "win", "wout"), None),
            P(None, ("win", "wout"), None, None),
            P(None, None, None, ("win", "wout")),
        ),
        check_vma=False,
    )
```

```python
import functools

import jax
import jax.numpy as jnp
from jax import lax
from jax.experimental import pallas as pl
from jax.experimental.pallas import tpu as pltpu
from jax.sharding import PartitionSpec as P

MESH = pl.DeviceIdType.MESH
DK = 128
CONV = 4
HALO = 16
F32 = jnp.float32
BF16 = jnp.bfloat16


def dot(a, b):
    return jnp.dot(a, b, preferred_element_type=F32)


def dot_t(a, b):
    return lax.dot_general(a, b, (((1,), (1,)), ((), ())), preferred_element_type=F32)


def split(x):
    high = x.astype(BF16)
    return high, (x - high.astype(F32)).astype(BF16)


def mm3(a, b):
    ah, al = split(a)
    bh, bl = split(b)
    return dot(ah, bh) + (dot(ah, bl) + dot(al, bh))


def mm1(a, b):
    return dot(a.astype(BF16), b.astype(BF16))


def mm_left(a, b):
    high, low = split(a)
    return dot(high, b) + dot(low, b)


def mm_right(a, b):
    high, low = split(b)
    return dot(a, high) + dot(a, low)


def kernel(
    n, wins, reqs,
    lengths, qkv, conv_w, beta, out_gain, hidden, norm_gain, w_out, w_qkv,
    qkv_next, stream_hbm, fs_hbm, edge_out,
    stream_out, fs_out, halo, wo_own, wo_sib, wq, state_send, state_recv, nh, nh_send, nh_recv,
    part_keep, part_send, part_recv, ns, gathered, proj_send, proj_recv,
    res, up_send, up_recv, down_send, down_recv,
    local_sem, halo_sem, wo_sem, state_sem, nh_sem, part_send_sem, part_recv_sem,
    ns_send_sem, ns_recv_sem, proj_send_sem, proj_recv_sem, up_sem, down_sem,
):
    rows = qkv.shape[1]
    width = qkv.shape[2]
    heads = width // DK
    half = rows // 2
    group = wins * 2
    blk = hidden.shape[0]
    k_idx = lax.axis_index("seq")
    w = lax.axis_index("win")
    c = lax.axis_index("wout")
    me = w * 2 + c
    sib = {"wout": 1 - c}
    above = {"seq": lax.rem(k_idx + 1, n)}
    below = {"seq": lax.rem(k_idx + n - 1, n)}
    not_first = k_idx > 0
    not_last = k_idx < n - 1

    def remote(src, dst, send_sem, recv_sem, device):
        return pltpu.make_async_remote_copy(
            src_ref=src, dst_ref=dst, send_sem=send_sem, recv_sem=recv_sem,
            device_id=device, device_id_type=MESH,
        )

    def peer(o):
        p = lax.rem(me + o, group)
        return p // 2, lax.rem(p, 2)

    barrier = pltpu.get_barrier_semaphore()
    for o in range(1, group):
        pw, pc = peer(o)
        pl.semaphore_signal(barrier, inc=1, device_id={"win": pw, "wout": pc}, device_id_type=MESH)

    @pl.when(not_first)
    def _():
        pl.semaphore_signal(barrier, inc=1, device_id=below, device_id_type=MESH)

    @pl.when(not_last)
    def _():
        pl.semaphore_signal(barrier, inc=1, device_id=above, device_id_type=MESH)

    copy_wo = pltpu.make_async_copy(w_out, wo_own, local_sem.at[0])
    copy_wq = pltpu.make_async_copy(w_qkv, wq, local_sem.at[1])
    copy_wo.start()
    copy_wq.start()
    ends = []
    total = jnp.int32(0)
    for r in range(reqs):
        total = total + lengths[r]
        ends.append(total)
    first = k_idx * rows

    def segments(positions):
        seg = jnp.zeros_like(positions)
        for r in range(reqs):
            seg = seg + (positions >= ends[r]).astype(jnp.int32)
        return jnp.where(positions < 0, -1, seg)

    def scalar_segment(position):
        seg = jnp.int32(0)
        for r in range(reqs):
            seg = seg + (position >= ends[r]).astype(jnp.int32)
        return jnp.where(position < 0, -1, seg)

    col_pos = first + lax.broadcasted_iota(jnp.int32, (rows, 1), 0)
    row_pos = first + lax.broadcasted_iota(jnp.int32, (1, rows), 1)
    col_seg = segments(col_pos)
    row_seg = segments(row_pos)
    before_seg = scalar_segment(first - 1)
    last_seg = scalar_segment(first + rows - 1)
    coupled = (col_seg == before_seg).astype(F32)
    in_last = (row_seg == last_seg).astype(F32)
    last_link = (before_seg == last_seg).astype(F32)

    ri = lax.broadcasted_iota(jnp.int32, (rows, rows), 0)
    ci = lax.broadcasted_iota(jnp.int32, (rows, rows), 1)
    same = col_seg == row_seg
    causal = same & (ri >= ci)
    strict = same & (ri > ci)
    diagonal = ri == ci
    hi_ = lax.broadcasted_iota(jnp.int32, (half, half), 0)
    hj_ = lax.broadcasted_iota(jnp.int32, (half, half), 1)
    eye_half = (hi_ == hj_).astype(F32)
    eye_keys = (
        lax.broadcasted_iota(jnp.int32, (DK, DK), 0) == lax.broadcasted_iota(jnp.int32, (DK, DK), 1)
    ).astype(F32)

    def silu(x):
        return (x / (1.0 + jnp.exp(-x))).astype(BF16).astype(F32)

    index_col = lax.broadcasted_iota(jnp.int32, (rows, 1), 0)
    keeps = [None] + [segments(col_pos - back) == col_seg for back in range(1, CONV)]

    def tap(t, back):
        return conv_w[t, CONV - 1 - back : CONV - back, :]

    pres = []
    mains = []
    def convolve(t):
        wide = qkv[t].astype(F32)
        pre = tap(t, 0) * wide
        for back in range(1, CONV):
            shifted = pltpu.roll(wide, back, axis=0)
            pre = pre + tap(t, back) * jnp.where(keeps[back] & (index_col >= back), shifted, 0.0)
        pres.append(pre[:8])
        mains.append(silu(pre)[8:])

    convolve(0)
    pl.semaphore_wait(
        barrier, group - 1 + not_first.astype(jnp.int32) + not_last.astype(jnp.int32)
    )

    halo_copy = remote(
        qkv.at[:, pl.ds(rows - HALO, HALO), :], halo, halo_sem.at[0], halo_sem.at[1], above
    )

    @pl.when(not_last)
    def _():
        halo_copy.start()

    wo_copy = remote(w_out, wo_sib, wo_sem.at[0], wo_sem.at[1], sib)
    wo_copy.start()

    @pl.when(jnp.logical_not(not_first))
    def _():
        halo[...] = jnp.zeros_like(halo)
        state_recv[...] = jnp.zeros_like(state_recv)

    convolve(1)
    convolve(2)
    strength = []
    for h in range(heads):
        b_row = 1.0 / (1.0 + jnp.exp(-beta[h : h + 1, :]))
        strength.append(jnp.sum(jnp.where(diagonal, b_row, 0.0), axis=1, keepdims=True))

    @pl.when(not_first)
    def _():
        halo_copy.wait_recv()

    activated = []
    for t in range(3):
        rim = halo[t].astype(F32)[HALO - 8 :]
        pre = pres[t]
        for back in range(1, CONV):
            shifted = pltpu.roll(rim, back, axis=0)
            pre = pre + tap(t, back) * jnp.where(
                keeps[back][:8] & (index_col[:8] < back), shifted, 0.0
            )
        activated.append(jnp.concatenate([silu(pre), mains[t]], axis=0))

    def norm_factor(x, axis):
        return lax.rsqrt(jnp.sum(x * x, axis=axis, keepdims=True) + 1e-6)

    q, k, v, kt, k_col, a_full, scores = [], [], [], [], [], [], []
    for h in range(heads):
        cols = slice(h * DK, (h + 1) * DK)
        q_raw, k_raw = activated[0][:, cols], activated[1][:, cols]
        q_col = norm_factor(q_raw, 1)
        k_col.append(norm_factor(k_raw, 1))
        kt_raw = jnp.transpose(k_raw)
        k_row = norm_factor(kt_raw, 0)
        q.append(q_raw * q_col)
        k.append(k_raw * k_col[h])
        v.append(activated[2][:, cols])
        kt.append(kt_raw)
        k_half = k_raw.astype(BF16)
        gram = dot_t(k_half, k_half) * k_row
        a_full.append(jnp.where(strict, (strength[h] * k_col[h]) * gram, 0.0))
        scores.append(
            jnp.where(causal, q_col * (dot_t(q_raw.astype(BF16), k_half) * k_row), 0.0)
        )

    diag = []
    for h in range(heads):
        diag.append(a_full[h][:half, :half])
        diag.append(a_full[h][half:, half:])
    level = 0
    inverse = None
    while (1 << level) < half:
        pick = (
            ((hi_ >> (level + 1)) == (hj_ >> (level + 1)))
            & (((hi_ >> level) & 1) == 1)
            & (((hj_ >> level) & 1) == 0)
        )
        lower = [jnp.where(pick, a, 0.0) for a in diag]
        if level == 0:
            inverse = [eye_half - x for x in lower]
        else:
            ys = [mm1(x, z) for x, z in zip(lower, inverse)]
            inverse = [z - mm1(z, y) for z, y in zip(inverse, ys)]
        level += 1

    solved, out_local, q_link, trans, write = [], [], [], [], []
    for h in range(heads):
        rhs = jnp.concatenate([strength[h] * v[h], (strength[h] * coupled) * k[h]], axis=1)
        top = mm3(inverse[2 * h], rhs[:half])
        low = mm3(inverse[2 * h + 1], rhs[half:] - mm1(a_full[h][half:, :half], top))
        solved.append(jnp.concatenate([top, low], axis=0))
    for h in range(heads):
        m = mm_right((kt[h] * in_last).astype(BF16), k_col[h] * solved[h])
        write.append(m[:, :DK])
        trans.append(last_link * (eye_keys - m[:, DK:]))

    steps = n // 2
    state_copies = [
        [
            remote(
                state_send.at[i, pl.ds(h * DK, DK)], state_recv.at[i, pl.ds(h * DK, DK)],
                state_sem.at[0, i * heads + h], state_sem.at[1, i * heads + h], above,
            )
            for h in range(heads)
        ]
        for i in range(steps)
    ]
    for i in range(steps):
        for h in range(heads):
            hr = slice(h * DK, (h + 1) * DK)
            state = write[h]
            if i > 0:
                pl.when(not_first)(state_copies[i - 1][h].wait_recv)
                state = state + mm_left(trans[h], state_recv[i - 1, hr, :])
            state_send[i, hr, :] = state.astype(BF16)
            pl.when(not_last)(state_copies[i][h].start)
        if i == 0:
            local = [mm1(scores[h], solved[h]) for h in range(heads)]
            links = [coupled * q[h] - local[h][:, DK:] for h in range(heads)]
    state_in = []

    corrected = []
    for h in range(heads):
        pl.when(not_first)(state_copies[steps - 1][h].wait_recv)
        state_in.append(state_recv[steps - 1, h * DK : (h + 1) * DK, :])
        att = local[h][:, :DK] + dot(links[h].astype(BF16), state_in[h])
        corrected.append(k_col[h] * (solved[h][:, :DK] - mm_left(solved[h][:, DK:], state_in[h])))
        scale = lax.rsqrt(jnp.mean(att * att, axis=-1, keepdims=True) + 1e-5)
        nh[:, h * DK : (h + 1) * DK] = (att * scale * out_gain[...]).astype(BF16)

    wy, wx = w // 2, lax.rem(w, 2)
    side, across, far = wy * 2 + (1 - wx), (1 - wy) * 2 + wx, 3 - w
    order = (w, side, across, far)

    def rows_for(pw, pc):
        return nh[pl.ds(pl.multiple_of((2 * pw + pc) * blk, blk), blk), :]

    for i, pw in enumerate(order):
        nh_send[i * blk : (i + 1) * blk, :] = rows_for(pw, 1 - c)
    nh_copy = remote(nh_send, nh_recv, nh_sem.at[0], nh_sem.at[1], sib)
    nh_copy.start()

    for r in range(reqs):
        owned = (ends[r] - 1 >= first) & (ends[r] - 1 < first + rows)
        owned_f = owned.astype(F32)
        member = (row_seg == r).astype(F32) * owned_f
        carry = owned_f * (before_seg == r).astype(F32)
        for h in range(heads):
            base = (r * heads + h) * DK
            res[base : base + DK, :] = (
                mm_right((kt[h] * member).astype(BF16), corrected[h])
                + carry * state_in[h].astype(F32)
            ).astype(BF16)
    edge_base = reqs * heads * DK

    def selection(base, count):
        sel_row = lax.broadcasted_iota(jnp.int32, (16, count), 0)
        sel_pos = base + lax.broadcasted_iota(jnp.int32, (16, count), 1)
        sel_seg = segments(sel_pos)
        select = jnp.zeros((16, count), F32)
        for r in range(reqs):
            owned = (ends[r] - 1 >= first) & (ends[r] - 1 < first + rows)
            for i in range(CONV - 1):
                hit = (
                    (sel_row == i * reqs + r)
                    & (sel_pos == ends[r] - (CONV - 1) + i)
                    & (sel_seg == r)
                )
                select = select + jnp.where(hit, 1.0, 0.0) * owned.astype(F32)
        return select.astype(BF16)

    select_halo = selection(first - HALO, HALO)
    select_own = selection(first, rows)
    pieces = width // DK
    for t in range(3):
        edge = dot(select_halo, halo[t]) + dot(select_own, qkv[t])
        for j in range(pieces):
            base = edge_base + (t * pieces + j) * 16
            res[base : base + 16, :] = edge[:, j * DK : (j + 1) * DK].astype(BF16)

    up_copy = remote(up_send, up_recv, up_sem.at[0], up_sem.at[1], above)
    down_copy = remote(down_send, down_recv, down_sem.at[0], down_sem.at[1], below)

    def up_step():
        up_copy.wait_recv()

        @pl.when(not_last)
        def _():
            up_send[...] = up_recv[...] + res[...]
            up_copy.start()

    def down_step():
        down_copy.wait_recv()

        @pl.when(not_first)
        def _():
            down_send[...] = down_recv[...] + res[...]
            down_copy.start()

    @pl.when(k_idx == 0)
    def _():
        up_recv[...] = jnp.zeros_like(up_recv)
        up_send[...] = res[...]
        up_copy.start()

    @pl.when(k_idx == n - 1)
    def _():
        down_recv[...] = jnp.zeros_like(down_recv)
        down_send[...] = res[...]
        down_copy.start()

    own_rows = jnp.concatenate([rows_for(pw, c) for pw in order], axis=0)
    copy_wo.wait()
    part_keep[...] = dot(own_rows, wo_own[...])
    wo_copy.wait_recv()
    nh_copy.wait_recv()

    def win_copies(send, recv, send_sem, recv_sem):
        return [
            remote(send.at[i], recv.at[i], send_sem.at[i], recv_sem.at[i], {"win": pw})
            for i, pw in enumerate((side, across) * 2 + (across, side))
        ]

    part_copies = win_copies(part_send, part_recv, part_send_sem, part_recv_sem)
    model = hidden.shape[1]
    part_cols = model // 2

    def relay(copies, send, recv, cols, far_term, side_term, across_term, own_term, between=None):
        term = far_term().astype(BF16)
        send[0] = term[:, :cols]
        copies[0].start()
        send[1] = term[:, cols:]
        copies[1].start()
        term = side_term()
        send[2] = term[:, :cols].astype(BF16)
        copies[2].start()
        side_rest = term[:, cols:]
        term = across_term()
        send[3] = term[:, cols:].astype(BF16)
        copies[3].start()
        across_rest = term[:, :cols]
        if between is not None:
            between()
        own = own_term()
        copies[0].wait_recv()
        send[4] = (across_rest + recv[0].astype(F32)).astype(BF16)
        copies[4].start()
        copies[1].wait_recv()
        send[5] = (side_rest + recv[1].astype(F32)).astype(BF16)
        copies[5].start()
        return own

    part_all = part_keep[...] + dot(nh_recv[...], wo_sib[...])
    part_terms = [part_all[i * blk : (i + 1) * blk] for i in range(wins)]
    own_part = relay(
        part_copies, part_send, part_recv, part_cols,
        lambda: part_terms[3], lambda: part_terms[1], lambda: part_terms[2],
        lambda: part_terms[0] + hidden[...].astype(F32),
    )

    for cp in part_copies[2:]:
        cp.wait_recv()
    summed = own_part + jnp.concatenate(
        [part_recv[2 + i].astype(F32) + part_recv[4 + i].astype(F32) for i in range(2)], axis=1
    )
    stream_out[...] = summed.astype(BF16)
    stream_copy = pltpu.make_async_copy(stream_out, stream_hbm, local_sem.at[2])
    stream_copy.start()
    scale = lax.rsqrt(jnp.mean(summed * summed, axis=-1, keepdims=True) + 1e-5)
    ns[...] = (summed * scale * norm_gain[...]).astype(BF16)
    in_block = wq.shape[0]
    my_rows = pl.ds(pl.multiple_of(me * blk, blk), blk)
    ns_copies = []
    for pw in (far, side, across):
        for pc in (c, 1 - c):
            i = len(ns_copies)
            cp = remote(
                ns.at[:, pl.ds(pl.multiple_of(pw * in_block, in_block), in_block)],
                gathered.at[my_rows, :],
                ns_send_sem.at[i], ns_recv_sem.at[i], {"win": pw, "wout": pc},
            )
            cp.start()
            ns_copies.append(cp)
    last = len(ns_copies)
    cp = remote(
        ns.at[:, pl.ds(pl.multiple_of(w * in_block, in_block), in_block)],
        gathered.at[my_rows, :],
        ns_send_sem.at[last], ns_recv_sem.at[last], sib,
    )
    cp.start()
    ns_copies.append(cp)
    gathered[my_rows, :] = ns[:, pl.ds(pl.multiple_of(w * in_block, in_block), in_block)]

    pl.when(k_idx == 1)(up_step)
    pl.when(k_idx == n - 2)(down_step)

    copy_wq.wait()
    out_rows = blk * 2
    cols = wq.shape[1] // 2

    def project(pw, arriving):
        for cp in arriving:
            cp.wait_recv()
        block = gathered[pl.ds(pl.multiple_of(pw * out_rows, out_rows), out_rows), :]
        return dot(block, wq[...])

    proj_copies = win_copies(proj_send, proj_recv, proj_send_sem, proj_recv_sem)
    def second_step():
        pl.when((k_idx == 2) & (k_idx > 1))(up_step)
        pl.when((k_idx == n - 3) & (k_idx < n - 2))(down_step)

    own = relay(
        proj_copies, proj_send, proj_recv, cols,
        lambda: project(far, ns_copies[0:2]), lambda: project(side, ns_copies[2:4]),
        lambda: project(across, ns_copies[4:6]), lambda: project(w, ns_copies[6:]),
        second_step,
    )

    pl.when(k_idx > 2)(up_step)
    pl.when(k_idx < n - 3)(down_step)

    total_res = res[...].astype(F32) + up_recv[...].astype(F32) + down_recv[...].astype(F32)
    fs_out[...] = total_res[:edge_base].astype(BF16)
    fs_copy = pltpu.make_async_copy(fs_out, fs_hbm, local_sem.at[3])
    fs_copy.start()
    for t in range(3 * pieces):
        base = edge_base + t * 16
        edge_out[:, t * DK : (t + 1) * DK] = total_res[base : base + 16]

    for cp in proj_copies[2:]:
        cp.wait_recv()
    for i, part in enumerate((slice(0, cols), slice(cols, 2 * cols))):
        qkv_next[:, part] = (
            own[:, part] + proj_recv[2 + i].astype(F32) + proj_recv[4 + i].astype(F32)
        ).astype(BF16)

    stream_copy.wait()
    fs_copy.wait()
    wo_copy.wait_send()
    nh_copy.wait_send()
    for cp in part_copies + ns_copies + proj_copies:
        cp.wait_send()

    @pl.when(not_last)
    def _():
        halo_copy.wait_send()
        for cp in [x for pair in state_copies for x in pair]:
            cp.wait_send()
        up_copy.wait_send()

    @pl.when(not_first)
    def _():
        down_copy.wait_send()


def place_results(
    reqs, taps, width,
    qkv_next, stream_out, states, edges,
    qkv_next_out, stream_out_out, states_out, edges_out,
    qkv_held, stream_held, states_held, states_wide, edges_held, sems,
):
    held = (qkv_held, stream_held, states_held)
    arrive = [
        pltpu.make_async_copy(src, dst, sems.at[i])
        for i, (src, dst) in enumerate(zip((qkv_next, stream_out, states), held))
    ]
    leave = [
        pltpu.make_async_copy(src, dst, sems.at[3 + i])
        for i, (src, dst) in enumerate(
            zip((qkv_held, stream_held, states_wide, edges_held), (qkv_next_out, stream_out_out, states_out, edges_out))
        )
    ]
    for i in (2, 0, 1):
        arrive[i].start()
    for i in range(taps):
        for t in range(3):
            edges_held[i, t] = edges[
                i * reqs : (i + 1) * reqs, t * width : (t + 1) * width
            ].astype(BF16)
    leave[3].start()
    arrive[2].wait()
    states_wide[...] = states_held[...].astype(F32)
    leave[2].start()
    for i in range(2):
        arrive[i].wait()
        leave[i].start()
    for cp in leave:
        cp.wait()


def solution(mesh):
    n, wins = mesh.shape["seq"], mesh.shape["win"]

    def body(qkv_in, conv_w, beta_logits, lengths, out_gain, w_out, hidden_in, norm_gain, w_qkv):
        rows, _, width = qkv_in.shape
        heads = width // DK
        reqs = lengths.shape[0]
        blk, model = hidden_in.shape
        in_block, out_cols = w_qkv.shape
        group = wins * 2
        res_rows = reqs * heads * DK + 16 * 3 * (width // DK)
        vmem = pl.BlockSpec(memory_space=pltpu.VMEM)
        place = pl.BlockSpec(memory_space=pl.ANY)
        dma = pltpu.SemaphoreType.DMA
        results = pl.pallas_call(
            functools.partial(kernel, n, wins, reqs),
            out_shape=(
                jax.ShapeDtypeStruct((blk * 2, out_cols), BF16),
                jax.ShapeDtypeStruct((blk, model), BF16),
                jax.ShapeDtypeStruct((reqs * heads * DK, DK), BF16),
                jax.ShapeDtypeStruct((16, 3 * width), F32),
            ),
            in_specs=[pl.BlockSpec(memory_space=pltpu.SMEM)] + [vmem] * 6
            + [pl.BlockSpec(memory_space=pl.ANY)] * 2,
            out_specs=(vmem, place, place, vmem),
            scratch_shapes=[
                pltpu.VMEM((blk, model), BF16),
                pltpu.VMEM((reqs * heads * DK, DK), BF16),
                pltpu.VMEM((3, HALO, width), BF16),
                pltpu.VMEM((width, model), BF16),
                pltpu.VMEM((width, model), BF16),
                pltpu.VMEM((in_block, out_cols), BF16),
                pltpu.VMEM((n // 2, heads * DK, DK), BF16),
                pltpu.VMEM((n // 2, heads * DK, DK), BF16),
                pltpu.VMEM((rows, width), BF16),
                pltpu.VMEM((rows // 2, width), BF16),
                pltpu.VMEM((rows // 2, width), BF16),
                pltpu.VMEM((rows // 2, model), F32),
                pltpu.VMEM((6, blk, model // 2), BF16),
                pltpu.VMEM((6, blk, model // 2), BF16),
                pltpu.VMEM((blk, model), BF16),
                pltpu.VMEM((rows, in_block), BF16),
                pltpu.VMEM((6, blk * 2, out_cols // 2), BF16),
                pltpu.VMEM((6, blk * 2, out_cols // 2), BF16),
                pltpu.VMEM((res_rows, DK), BF16),
                pltpu.VMEM((res_rows, DK), BF16),
                pltpu.VMEM((res_rows, DK), BF16),
                pltpu.VMEM((res_rows, DK), BF16),
                pltpu.VMEM((res_rows, DK), BF16),
                dma((4,)), dma((2,)), dma((2,)), dma((2, n // 2 * heads)), dma((2,)),
                dma((6,)), dma((6,)), dma((group,)), dma((group,)),
                dma((6,)), dma((6,)), dma((2,)), dma((2,)),
            ],
            compiler_params=pltpu.CompilerParams(
                collective_id=0, has_side_effects=True, vmem_limit_bytes=56 * 1024 * 1024
            ),
            cost_estimate=pl.CostEstimate(
                flops=4 * 10**9, bytes_accessed=8 * 10**6, transcendentals=10**6
            ),
            name="delta_sublayer",
        )(
            lengths, jnp.transpose(qkv_in, (1, 0, 2)), conv_w, beta_logits,
            out_gain.reshape(1, DK), hidden_in, norm_gain.reshape(1, model), w_out, w_qkv,
        )
        taps = CONV - 1
        projected, stream, states, edges = pl.pallas_call(
            functools.partial(place_results, reqs, taps, width),
            out_shape=tuple(jax.ShapeDtypeStruct(x.shape, x.dtype) for x in results[:2])
            + (jax.ShapeDtypeStruct(results[2].shape, F32),)
            + (jax.ShapeDtypeStruct((taps, 3, reqs, width), BF16),),
            in_specs=[place] * 3 + [vmem],
            out_specs=(place,) * 4,
            scratch_shapes=[pltpu.VMEM(x.shape, x.dtype) for x in results[:3]]
            + [pltpu.VMEM(results[2].shape, F32)]
            + [pltpu.VMEM((taps, 3, reqs, width), BF16), dma((7,))],
            compiler_params=pltpu.CompilerParams(vmem_limit_bytes=60 * 1024 * 1024),
            name="place_results",
        )(*results)
        return projected, stream, states.reshape(reqs, heads, DK, DK), jnp.transpose(edges, (2, 0, 1, 3))

    return jax.shard_map(
        body,
        mesh=mesh,
        in_specs=(
            P("seq", None, ("win", "wout")),
            P(None, None, ("win", "wout")),
            P(("win", "wout"), "seq"),
            P(),
            P(),
            P(("win", "wout"), None),
            P(("seq", "win", "wout"), None),
            P(),
            P("win", "wout"),
        ),
        out_specs=(
            P(("seq", "win"), "wout"),
            P(("seq", "win", "wout"), None),
            P(None, ("win", "wout"), None, None),
            P(None, None, None, ("win", "wout")),
        ),
        check_vma=False,
    )
```
